256 devices in a mesh: dp: 16 (over z_lo, x), ctx: 16 (over y, z_hi, core).
Axes of the slice: x: 4, y: 4, z: 8 (z_hi: 2, z_lo: 4; z = z_hi * 4 + z_lo), core: 2. Of those that a mesh axis runs over, the one named last changes fastest.
Arguments:
- queries: bfloat16 [32768, 32, 128], P(('dp', 'ctx')), may hold values from -8 to 8
- keys: bfloat16 [32768, 4, 128], P(('dp', 'ctx')), may hold values from -8 to 8
- values: bfloat16 [32768, 4, 128], P(('dp', 'ctx')), may hold values from -6 to 6
- out_grad: bfloat16 [32768, 32, 128], P(('dp', 'ctx')), may hold values from -6 to 6
- q_gain: float32 [128], replicated, may hold values from 0.5 to 5
- k_gain: float32 [128], replicated, may hold values from 0.5 to 5
- lengths: int32 [16, 8], P('dp'), may hold values from 1 to 1025, 2048 in all within a row
- prompt_ids: int32 [16, 8], replicated, may hold values from 0 to 15, as said below
- grades: int32 [16, 8], replicated, may hold values from 0 to 3
Outputs:
- q_grad: bfloat16 [32768, 32, 128], P(('dp', 'ctx'))
- k_grad: bfloat16 [32768, 4, 128], P(('dp', 'ctx'))
- v_grad: bfloat16 [32768, 4, 128], P(('dp', 'ctx'))
- q_gain_grad: float32 [128], replicated
- k_gain_grad: float32 [128], replicated
The draws below stay inside these ranges and needn't reach their ends.
Inputs may be any that keep to these rules, and one draw needn't show every extreme that they name: Each row's lengths sum to 2048; the longest response of each row has 1025 tokens. `prompt_ids`: every id names exactly 8 responses.
All inputs are finite; a program needn't handle non-finite values.
Results may differ from the reference program's by a relative error of at most 0.004.
The reference program's roundings to bfloat16 on the way (of `dout`) count: a program that leaves them out, or rounds other values in their place, can miss the bound.
Values may be sent and summed in bfloat16 or wider, within the bound.
No kernel may reach another device: no remote copies, remote signals or barrier semaphores. Data moves between devices by JAX's collectives and lax.ppermute only.
A program may use at most 128 MiB of HBM per device.

```python
import math
import jax
import jax.numpy as jnp
import numpy as np
from jax import lax

HQ = 32
HK = 4
HD = 128
SEGS = 8
REWRITES = 8
ROW = 2048
TOKENS = 32768
N_DP = 16


def draw_queries(key, part):
    key = jax.random.fold_in(key, 1)
    base = jnp.clip(jax.random.normal(key, (TOKENS, HQ, HD), jnp.float32), -6.0, 6.0)
    return jnp.clip(base, -8.0, 8.0).astype(jnp.bfloat16)


def draw_keys(key, part):
    key = jax.random.fold_in(key, 2)
    base = jnp.clip(jax.random.normal(key, (TOKENS, HK, HD), jnp.float32), -6.0, 6.0)
    return jnp.clip(base, -8.0, 8.0).astype(jnp.bfloat16)


def gain_values(key):
    drawn = jax.random.uniform(key, (HD,), jnp.float32, 0.5, 2.0)
    return drawn


def draw_q_gain(key, part):
    key = jax.random.fold_in(key, 3)
    return gain_values(key)


def draw_k_gain(key, part):
    key = jax.random.fold_in(key, 4)
    return gain_values(key)


def draw_prompt_ids(key, part):
    key = jax.random.fold_in(key, 6)
    shuffled = jax.random.permutation(key, N_DP * SEGS).astype(jnp.int32)
    return (shuffled // REWRITES).reshape(N_DP, SEGS).astype(jnp.int32)


def plant(values, key, least, top_value):
    index_at = [jax.random.randint(jax.random.fold_in(key, axis), (), 0, length) for axis, length in enumerate(values.shape)]
    main_axis = values.shape.index(max(values.shape))
    next_to = index_at[:main_axis] + [(index_at[main_axis] + 1) % values.shape[main_axis]] + index_at[main_axis + 1:]
    return values.at[tuple(index_at)].set(least).at[tuple(next_to)].set(top_value)


def levels(rng, shape, cuts, smallest, high):
    level = 1.0
    for dim, parts in cuts:
        steps = jax.random.uniform(jax.random.fold_in(jax.random.fold_in(rng, 6), dim), (parts,), jnp.float32, smallest / len(cuts), high / len(cuts))
        level = level * jnp.repeat(jnp.exp(steps), shape[dim] // parts).reshape((-1,) + (1,) * (len(shape) - 1 - dim))
    return level


def length_profile(number_of, total, limit, slope):
    weights = [(1 << 20) // math.isqrt(standing ** slope) + 1 for standing in range(2, number_of + 1)]
    surplus, counts = total - limit - (number_of - 1), [1] * (number_of - 1)
    while surplus > 0:
        movable = [i for i in range(number_of - 1) if counts[i] < limit]
        whole, left = sum([weights[i] for i in movable]), surplus
        for i in movable:
            extra = min(limit - counts[i], max(1, left * weights[i] // whole), surplus)
            counts[i] = counts[i] + extra
            surplus = surplus - extra
    return np.array([limit] + counts)


def ragged(stream_key, count, total, limit, skew):
    if count == 2:
        one = jax.random.randint(stream_key, (), max(1, total - limit), min(limit, total - 1) + 1)
        return jnp.stack([one, total - one])
    sizes = jnp.asarray(length_profile(count, total, limit, skew), jnp.int32)
    pairs = (count - 1) // 2
    source_of, sink = sizes[1:1 + 2 * pairs:2], sizes[2:2 + 2 * pairs:2]
    margin = jnp.minimum(source_of - 1, limit - sink)
    shifted = jax.random.randint(jax.random.fold_in(stream_key, 1), (pairs,), 0, 1 << 20) % (margin + 1)
    sizes = sizes.at[1:1 + 2 * pairs:2].set(source_of - shifted).at[2:2 + 2 * pairs:2].set(sink + shifted)
    return sizes[jax.random.permutation(jax.random.fold_in(stream_key, 2), count)]


def centred(rng, extent, deviation, reach, pieces=(), kind=jnp.bfloat16):
    values = jax.random.normal(rng, extent, jnp.float32) * deviation
    if len(pieces) > 0:
        values = levels(rng, extent, pieces, -0.22, 0.18) * values
    return jnp.clip(values, min=-reach, max=reach).astype(kind)


def setup_inputs(seed: int = 0) -> dict:
    key_of = jax.random.split(jax.random.key(seed), 10)
    return {
        "queries": draw_queries(jax.random.fold_in(key_of[9], 71), 0),
        "keys": draw_keys(jax.random.fold_in(key_of[9], 71), 0),
        "values": centred(key_of[2], (TOKENS, HK, HD), 1.0, 6.0, ((0, 256),)),
        "out_grad": centred(key_of[3], (TOKENS, HQ, HD), 1.0, 6.0, ((0, 256),)),
        "q_gain": draw_q_gain(jax.random.fold_in(key_of[9], 71), 0),
        "k_gain": draw_k_gain(jax.random.fold_in(key_of[9], 71), 0),
        "lengths": jax.vmap(lambda own: ragged(own, SEGS, ROW, ROW // 2 + 1, 2))(jax.random.split(key_of[6], N_DP)).reshape((N_DP, SEGS)).astype(jnp.int32),
        "prompt_ids": draw_prompt_ids(jax.random.fold_in(key_of[9], 71), 0),
        "grades": plant(jax.random.randint(key_of[8], (N_DP, SEGS), 0, 4), jax.random.fold_in(key_of[8], 1), 0, 3).astype(jnp.int32),
    }


norm_eps = 1e-06

def layout(lens):
    ends = jnp.cumsum(lens).astype(jnp.int32)
    starts = (ends - lens).astype(jnp.int32)
    index = jnp.arange(ROW, dtype=jnp.int32)
    member = lax.optimization_barrier(jnp.sum((index[:, None] >= ends[None, :]).astype(jnp.int32), axis=1)).astype(jnp.int32)
    owners = member[:, None] == jnp.arange(lens.shape[0], dtype=jnp.int32)[None, :]
    opening = lax.optimization_barrier(jnp.sum(jnp.where(owners, starts[None, :], 0), axis=1)).astype(jnp.int32)
    return (member, (index - opening).astype(jnp.int32))

def advantages(grades, prompt_ids):
    graded = grades.reshape(-1).astype(jnp.float32)
    labels = prompt_ids.reshape(-1)
    same = (labels[:, None] == labels[None, :]).astype(jnp.float32)
    counted = lax.optimization_barrier(jnp.sum(same, axis=1))
    centre = lax.optimization_barrier(jnp.sum(same * graded[None, :], axis=1)) / counted
    spread = graded[None, :] - centre[:, None]
    variance = lax.optimization_barrier(jnp.sum(same * spread * spread, axis=1)) / counted
    return ((graded - centre) / jnp.maximum(jnp.sqrt(variance), 1.0)).reshape(grades.shape)

def rope_tables(positions, head_width):
    half = head_width // 2
    freqs = jnp.power(1000000.0, -(jnp.arange(half, dtype=jnp.float32) * (2.0 / head_width)))
    angles = positions.astype(jnp.float32)[:, None] * freqs[None, :]
    cosine = jnp.cos(angles)
    sine = jnp.sin(angles)
    return (jnp.concatenate([cosine, cosine], axis=1), jnp.concatenate([sine, sine], axis=1))

def norm_rope(inputs, gain, cosine, sine):
    values_f = inputs.astype(jnp.float32)
    inv_rms = lax.rsqrt(lax.optimization_barrier(jnp.mean(values_f * values_f, axis=-1, keepdims=True)) + norm_eps)
    normed = values_f * inv_rms * gain
    half = inputs.shape[-1] // 2
    turned = jnp.concatenate([-normed[..., half:], normed[..., :half]], axis=-1)
    return (normed * cosine[:, None, :] + turned * sine[:, None, :]).astype(jnp.bfloat16)

def unrotate(inputs, gain, cosine, sine, incoming):
    half = inputs.shape[-1] // 2
    along = incoming * cosine[:, None, :]
    across = incoming * sine[:, None, :]
    d_normed = along - jnp.concatenate([-across[..., half:], across[..., :half]], axis=-1)
    values_f = inputs.astype(jnp.float32)
    inv_rms = lax.rsqrt(lax.optimization_barrier(jnp.mean(values_f * values_f, axis=-1, keepdims=True)) + norm_eps)
    unit = values_f * inv_rms
    gain_term = lax.optimization_barrier(jnp.sum(d_normed * unit, axis=(0, 1)))
    upper = d_normed * gain
    result = inv_rms * (upper - unit * lax.optimization_barrier(jnp.mean(upper * unit, axis=-1, keepdims=True)))
    return (result.astype(jnp.bfloat16), gain_term)

def head_grads(bundle):
    query_part, key_part, value_part, grad_part, member = bundle
    inv_root = 1.0 / math.sqrt(HD)
    query_f = query_part.astype(jnp.float32)
    key_f = key_part.astype(jnp.float32)
    value_f = value_part.astype(jnp.float32)
    grad_f = grad_part.astype(jnp.float32)
    index = jnp.arange(ROW, dtype=jnp.int32)
    allowed = (member[:, None] == member[None, :]) & (index[None, :] <= index[:, None])
    score = jnp.einsum('qgd,kd->gqk', query_f, key_f) * inv_root
    masked = jnp.where(allowed[None], score, -1e+30)
    peak = lax.optimization_barrier(jnp.max(masked, axis=-1, keepdims=True))
    weights = jnp.where(allowed[None], jnp.exp(masked - peak), 0.0)
    log_total = peak + jnp.log(lax.optimization_barrier(jnp.sum(weights, axis=-1, keepdims=True)))
    prob = jnp.where(allowed[None], jnp.exp(masked - log_total), 0.0)
    d_prob = jnp.einsum('qgd,kd->gqk', grad_f, value_f)
    d_total = lax.optimization_barrier(jnp.sum(prob * d_prob, axis=-1, keepdims=True))
    d_score = lax.optimization_barrier((prob * (d_prob - d_total)).astype(jnp.bfloat16)).astype(jnp.float32)
    prob_b = lax.optimization_barrier(prob.astype(jnp.bfloat16)).astype(jnp.float32)
    value_grad = jnp.einsum('gqk,qgd->kd', prob_b, grad_f)
    query_grad = jnp.einsum('gqk,kd->qgd', d_score, key_f) * inv_root
    key_grad = jnp.einsum('gqk,qgd->kd', d_score, query_f) * inv_root
    return (query_grad, key_grad, value_grad)

def reference(queries, keys, values, out_grad, q_gain, k_gain, lengths, prompt_ids, grades):
    member, positions = jax.vmap(layout)(lengths)
    adv = advantages(grades, prompt_ids)
    weight = jnp.take_along_axis(adv, member, axis=1).reshape(-1)
    dout = (weight[:, None, None] * out_grad.astype(jnp.float32)).astype(jnp.bfloat16)
    cosine, sine = rope_tables(positions.reshape(-1), HD)
    q_rot = norm_rope(queries, q_gain, cosine, sine)
    k_rot = norm_rope(keys, k_gain, cosine, sine)
    group_size = HQ // HK

    def split_heads(array, width_heads):
        shaped = array.reshape(N_DP, ROW, HK, width_heads, HD).transpose(0, 2, 1, 3, 4)
        return shaped.reshape(N_DP * HK, ROW, width_heads, HD)
    query_stack = split_heads(q_rot, group_size)
    grad_stack = split_heads(dout, group_size)
    key_stack = split_heads(k_rot, 1)[:, :, 0]
    value_stack = split_heads(values, 1)[:, :, 0]
    member_stack = jnp.repeat(member, HK, axis=0)
    dq_stack, dk_stack, dv_stack = lax.map(head_grads, (query_stack, key_stack, value_stack, grad_stack, member_stack))
    dq_all = dq_stack.reshape(N_DP, HK, ROW, group_size, HD).transpose(0, 2, 1, 3, 4).reshape(TOKENS, HQ, HD)
    dk_all = dk_stack.reshape(N_DP, HK, ROW, HD).transpose(0, 2, 1, 3).reshape(TOKENS, HK, HD)
    dv_all = dv_stack.reshape(N_DP, HK, ROW, HD).transpose(0, 2, 1, 3).reshape(TOKENS, HK, HD)
    q_grad, q_term = unrotate(queries, q_gain, cosine, sine, dq_all)
    k_grad, k_term = unrotate(keys, k_gain, cosine, sine, dk_all)
    return (q_grad, k_grad, dv_all.astype(jnp.bfloat16), q_term, k_term)
```

```python
import functools
import math

import jax
import jax.numpy as jnp
from jax import lax
from jax.experimental import pallas as pl
from jax.experimental.pallas import tpu as pltpu
from jax.sharding import PartitionSpec as P

EPS = 1e-06
TOK = 128
HD = 128
BLK = 2 * TOK
REACH = 4
GROUP = 8
HEADS = 2
SLOTS = HEADS * 2 * (GROUP // 2)
ROOT = 1.0 / math.sqrt(HD)
EXP_SCALE = ROOT * math.log2(math.e)
MASKED = -1e30
QMAX = 32000.0
VMEM = pltpu.CompilerParams(vmem_limit_bytes=56 * 1024 * 1024)

f32, bf16, i32 = jnp.float32, jnp.bfloat16, jnp.int32


def dot(a, b, dims):
    return lax.dot_general(a, b, (dims, ((), ())), preferred_element_type=f32)


def inv_rms(x):
    return lax.rsqrt(jnp.mean(x * x, axis=-1, keepdims=True) + EPS)


def turn(x):
    return pltpu.roll(x, HD // 2, x.ndim - 1)


def norm_rope(x, gain, cosine, sine):
    xn = x * inv_rms(x) * gain
    return xn * cosine + turn(xn) * sine


def unrotate(x, gain, cosine, sine, incoming):
    dn = incoming * cosine - turn(incoming) * sine
    r = inv_rms(x)
    unit = x * r
    u = dn * gain
    grad = r * (u - unit * jnp.mean(u * unit, axis=-1, keepdims=True))
    return grad, jnp.sum(dn * unit, axis=0, keepdims=True)


def token_base(place, k, half):
    chip, core = place // 2, place % 2
    return ((chip - k) * 2 + (core if half == 0 else 1 - core)) * TOK


def openings(idx, lens):
    total = jnp.int32(0)
    out = jnp.zeros_like(idx)
    for j in range(lens.shape[1]):
        total = total + lens[0, j]
        out = jnp.where(idx >= total, total, out)
    return out


def needed(place, k, half, lens):
    base = token_base(place, 0, half)
    total, first = jnp.int32(0), jnp.int32(0)
    for j in range(lens.shape[1]):
        total = total + lens[0, j]
        first = jnp.where(base >= total, total, first)
    low = (place // 2 - k) * BLK
    return (low >= 0) & (low + BLK > first)


def fill_bias(bias, place, k, half, lens):
    qidx = token_base(place, 0, half) + lax.broadcasted_iota(i32, (1, TOK), 1)
    start = openings(qidx, lens)
    for part in range(2):
        kidx = token_base(place, k, part) + lax.broadcasted_iota(i32, (TOK, TOK), 0)
        good = (kidx <= qidx) & (kidx >= start)
        row = jnp.where(good, 0.0, MASKED)
        bias[part * TOK : (part + 1) * TOK, :] = jnp.concatenate([row, row], axis=1)


def place_of():
    return lax.axis_index("ctx")


def prep_kernel(
    lens, ids_s, grades_s, ids, grades, q_own, q_other, g_own, g_other, gain, cosine, sine, q_out, g_out
):
    place, row, core = place_of(), lax.axis_index("dp"), lax.axis_index("ctx") % 2
    gain_row = gain[...]
    adv = []
    pid, grd = ids[...], grades[...].astype(f32)
    for j in range(lens.shape[1]):
        same = jnp.where(pid == ids_s[row, j], 1.0, 0.0)
        count = jnp.sum(same, keepdims=True)
        centre = jnp.sum(same * grd, keepdims=True) / count
        spread = grd - centre
        variance = jnp.sum(same * spread * spread, keepdims=True) / count
        own = grades_s[row, j].astype(f32)
        adv.append((own - centre) / jnp.maximum(jnp.sqrt(variance), 1.0))
    for half in range(2):
        idx = token_base(place, 0, half) + lax.broadcasted_iota(i32, (TOK, HD), 0)
        weight = jnp.zeros((TOK, HD), f32)
        total = jnp.int32(0)
        for j in range(lens.shape[1]):
            weight = jnp.where(idx >= total, adv[j], weight)
            total = total + lens[0, j]
        cos_h = cosine[0, half * TOK : (half + 1) * TOK, :]
        sin_h = sine[0, half * TOK : (half + 1) * TOK, :]

        def body(pair, carry):
            head, two = pair // (GROUP // 2), pair % (GROUP // 2)
            slot = (head * 2 + half) * (GROUP // 2) + two
            for e in range(2):
                n = pair * 2 + e
                if half == 0:
                    x, g = q_own[core, n], g_own[core, n]
                else:
                    x, g = q_other[n], g_other[n]
                rot = norm_rope(x.astype(f32), gain_row, cos_h, sin_h)
                q_out[slot, e * TOK : (e + 1) * TOK, :] = rot.astype(bf16)
                g_out[slot, e * TOK : (e + 1) * TOK, :] = (weight * g.astype(f32)).astype(bf16)
            return carry

        lax.fori_loop(0, HEADS * GROUP // 2, body, 0)


def rotate_keys(kv, gain_row, cosine, sine, kr):
    for half in range(2):
        rows = slice(half * TOK, (half + 1) * TOK)
        for head in range(HEADS):
            x = kv[half, 0, head].astype(f32)
            kr[head, rows, :] = norm_rope(x, gain_row, cosine[rows, :], sine[rows, :]).astype(bf16)


def join_values(kv, vv):
    for half in range(2):
        for head in range(HEADS):
            vv[head, half * TOK : (half + 1) * TOK, :] = kv[half, 1, head]


def forward_kernel(blocks, has_state, *refs):
    lens, gain, cosine, sine, q, g = refs[:6]
    rest = refs[6:]
    kvs, rest = rest[: len(blocks)], rest[len(blocks) :]
    if has_state:
        old, rest = rest[:3], rest[3:]
    (m, l, d), (kr, vv, bias) = rest[:3], rest[3:]
    place = place_of()
    gain_row = gain[...]
    if has_state:
        m[...], l[...], d[...] = old[0][...], old[1][...], old[2][...]
    else:
        m[...] = jnp.full(m.shape, MASKED, f32)
        l[...] = jnp.zeros(l.shape, f32)
        d[...] = jnp.zeros(d.shape, f32)
    for k, kv in zip(blocks, kvs):
        rotate_keys(kv, gain_row, cosine.at[k], sine.at[k], kr)
        join_values(kv, vv)
        for half in range(2):

            @pl.when(needed(place, k, half, lens))
            def _():
                fill_bias(bias, place, k, half, lens)

                def body(it, carry):
                    head, two = it // (GROUP // 2), it % (GROUP // 2)
                    slot = (head * 2 + half) * (GROUP // 2) + two
                    s = dot(kr[head], q[slot], ((1,), (1,))) + bias[...]
                    dp = dot(vv[head], g[slot], ((1,), (1,)))
                    m_old = m[slot]
                    m_new = jnp.maximum(m_old, jnp.max(s, axis=0, keepdims=True))
                    e = jnp.exp2((s - m_new) * EXP_SCALE)
                    fade = jnp.exp2((m_old - m_new) * EXP_SCALE)
                    m[slot] = m_new
                    l[slot] = l[slot] * fade + jnp.sum(e, axis=0, keepdims=True)
                    d[slot] = d[slot] * fade + jnp.sum(e * dp, axis=0, keepdims=True)
                    return carry

                lax.fori_loop(0, HEADS * GROUP // 2, body, 0)


def code(dk, dv, packed):
    rows = lax.broadcasted_iota(i32, (16, HD), 0)
    marks = jnp.zeros((16, HD), f32)
    for kind, ref in enumerate((dk, dv)):
        for head in range(HEADS):
            x = ref[head]
            peak = jnp.maximum(jnp.max(jnp.abs(x), axis=0, keepdims=True), 1e-30)
            mark = jnp.ceil(jnp.log2(peak) * 256.0)
            n = kind * HEADS + head
            marks = jnp.where(rows == n, mark, marks)
            fixed = x * (jnp.exp2(mark * (-1.0 / 256.0)) * QMAX)
            packed[n * BLK : (n + 1) * BLK, :] = (
                jnp.floor(fixed + 0.5).astype(i32).astype(jnp.int16)
            )
    packed[2 * HEADS * BLK :, :] = marks.astype(i32).astype(jnp.int16)


def backward_kernel(blocks, has_dq, last, *refs):
    lens, gain, cosine, sine, q, g, m, l, d = refs[:9]
    rest = refs[9:]
    kvs, rest = rest[: len(blocks)], rest[len(blocks) :]
    if has_dq:
        dq_in, term_in, rest = rest[0], rest[1], rest[2:]
    if last:
        (q_own, q_other, q_gain), rest = rest[:3], rest[3:]
        (q_grad, terms, dk_own, dv_own), rest = rest[:4], rest[4:]
        dq, kr, vv, krt, bias, dk, dv, lse, mean_d = rest
        packs = ()
    else:
        (dq, terms), rest = rest[:2], rest[2:]
        packs, rest = rest[: len(blocks)], rest[len(blocks) :]
        kr, vv, krt, bias, dk, dv, lse, mean_d = rest
    place, core = place_of(), lax.axis_index("ctx") % 2
    gain_row = gain[...]
    if has_dq:
        dq[...] = dq_in[...]
        terms[...] = term_in[...]
    else:
        dq[...] = jnp.zeros(dq.shape, f32)
        terms[...] = jnp.zeros(terms.shape, f32)
    lse[...] = m[...] * EXP_SCALE + jnp.log2(l[...])
    mean_d[...] = d[...] / l[...]
    for n, (k, kv) in enumerate(zip(blocks, kvs)):
        if last:
            dk, dv = dk_own, dv_own
        dk[...] = jnp.zeros(dk.shape, f32)
        dv[...] = jnp.zeros(dv.shape, f32)
        rotate_keys(kv, gain_row, cosine.at[k], sine.at[k], kr)
        join_values(kv, vv)
        for head in range(HEADS):
            krt[head] = jnp.transpose(kr[head].astype(f32)).astype(bf16)
        for half in range(2):

            @pl.when(needed(place, k, half, lens))
            def _():
                fill_bias(bias, place, k, half, lens)

                def body(it, carry):
                    head, two = it // (GROUP // 2), it % (GROUP // 2)
                    slot = (head * 2 + half) * (GROUP // 2) + two
                    s = dot(kr[head], q[slot], ((1,), (1,))) + bias[...]
                    dp = dot(vv[head], g[slot], ((1,), (1,)))
                    p = jnp.exp2(s * EXP_SCALE - lse[slot])
                    ds = (p * (dp - mean_d[slot])).astype(bf16)
                    dv[head] += dot(p.astype(bf16), g[slot], ((1,), (0,)))
                    dk[head] += dot(ds, q[slot], ((1,), (0,)))
                    dq[slot] += dot(krt[head], ds, ((1,), (0,)))
                    return carry

                lax.fori_loop(0, HEADS * GROUP // 2, body, 0)

        total = jnp.zeros((1, HD), f32)
        for half in range(2):
            rows = slice(half * TOK, (half + 1) * TOK)
            for head in range(HEADS):
                x = kv[half, 0, head].astype(f32)
                dn = (
                    dk[head, rows, :] * cosine[k, rows, :] - turn(dk[head, rows, :]) * sine[k, rows, :]
                )
                total = total + jnp.sum(dn * (x * inv_rms(x)), axis=0, keepdims=True)
        terms[1:2, :] = terms[1:2, :] + total * ROOT
        if not last:
            code(dk, dv, packs[n])
    if last:
        for half in range(2):
            cos_h = cosine[0, half * TOK : (half + 1) * TOK, :]
            sin_h = sine[0, half * TOK : (half + 1) * TOK, :]

            def finish(pair, total):
                head, two = pair // (GROUP // 2), pair % (GROUP // 2)
                slot = (head * 2 + half) * (GROUP // 2) + two
                incoming = jnp.transpose(dq[slot]) * ROOT
                for e in range(2):
                    n = pair * 2 + e
                    x = (q_own[core, n] if half == 0 else q_other[n]).astype(f32)
                    grad, part = unrotate(
                        x, q_gain[...], cos_h, sin_h, incoming[e * TOK : (e + 1) * TOK, :]
                    )
                    q_grad[half, n] = grad.astype(bf16)
                    total = total + part
                return total

            total = lax.fori_loop(0, HEADS * GROUP // 2, finish, jnp.zeros((1, HD), f32))
            terms[0:1, :] = terms[0:1, :] + total


def finish_kernel(gain, cosine, sine, kv, dk, dv, p1, p2, p3, p4, out):
    gain_row = gain[...]
    packs = (p1, p2, p3, p4)
    marks = [p[2 * HEADS * BLK :, :].astype(i32).astype(f32) for p in packs]
    for kind, ref in enumerate((dk, dv)):
        for head in range(HEADS):
            n = kind * HEADS + head
            scales = [jnp.exp2(k[n : n + 1, :] * (1.0 / 256.0)) * (1.0 / QMAX) for k in marks]
            for half in range(2):
                rows = slice(half * TOK, (half + 1) * TOK)
                total = ref[head, rows, :]
                for p, scale in zip(packs, scales):
                    at = n * BLK + half * TOK
                    total = total + p[at : at + TOK, :].astype(i32).astype(f32) * scale
                if kind == 0:
                    x = kv[half, 0, head].astype(f32)
                    total, _ = unrotate(
                        x, gain_row, cosine[0, rows, :], sine[0, rows, :], total * ROOT
                    )
                out[half, kind, head] = total.astype(bf16)


def vmem(count):
    return [pl.BlockSpec(memory_space=pltpu.VMEM)] * count


def smem(count):
    return [pl.BlockSpec(memory_space=pltpu.SMEM)] * count


def block_scratch():
    return [
        pltpu.VMEM((HEADS, BLK, HD), bf16),
        pltpu.VMEM((HEADS, BLK, HD), bf16),
    ]


def bias_scratch():
    return pltpu.VMEM((BLK, BLK), f32)


STAT = jax.ShapeDtypeStruct((SLOTS, 1, BLK), f32)


def cost(units, flops):
    return pl.CostEstimate(
        flops=units * flops, bytes_accessed=4 << 20, transcendentals=units * BLK * BLK
    )


def forward(blocks, lens, gain, cosine, sine, q, g, kvs, state):
    has_state = state is not None
    args = [lens, gain, cosine, sine, q, g, *kvs, *(state or ())]
    return pl.pallas_call(
        functools.partial(forward_kernel, blocks, has_state),
        out_shape=[STAT] * 3,
        in_specs=smem(1) + vmem(len(args) - 1),
        out_specs=vmem(3),
        scratch_shapes=block_scratch() + [bias_scratch()],
        compiler_params=VMEM,
        cost_estimate=cost(16 * len(blocks), 4 * BLK * BLK * HD),
        name="forward" + "".join(map(str, blocks)),
    )(*args)


def backward(blocks, lens, gain, cosine, sine, q, g, state, kvs, carried, final):
    has_dq, last = carried is not None, final is not None
    args = [lens, gain, cosine, sine, q, g, *state, *kvs, *(carried or ()), *(final or ())]
    dq = (SLOTS, HD, BLK)
    terms = jax.ShapeDtypeStruct((8, HD), f32)
    grads = (HEADS, BLK, HD)
    scratch = block_scratch() + [pltpu.VMEM((HEADS, HD, BLK), bf16), bias_scratch()]
    scratch += [pltpu.VMEM(grads, f32)] * 2 + [pltpu.VMEM((SLOTS, 1, BLK), f32)] * 2
    if last:
        out_shape = [
            jax.ShapeDtypeStruct((2, HEADS * GROUP, TOK, HD), bf16),
            terms,
            jax.ShapeDtypeStruct(grads, f32),
            jax.ShapeDtypeStruct(grads, f32),
        ]
        scratch = [pltpu.VMEM(dq, f32)] + scratch
    else:
        packed = jax.ShapeDtypeStruct((2 * HEADS * BLK + 16, HD), jnp.int16)
        out_shape = [jax.ShapeDtypeStruct(dq, f32), terms] + [packed] * len(blocks)
    return pl.pallas_call(
        functools.partial(backward_kernel, blocks, has_dq, last),
        out_shape=out_shape,
        in_specs=smem(1) + vmem(len(args) - 1),
        out_specs=vmem(len(out_shape)),
        scratch_shapes=scratch,
        compiler_params=VMEM,
        cost_estimate=cost(16 * len(blocks), 10 * BLK * BLK * HD),
        name="backward" + "".join(map(str, blocks)),
    )(*args)


def rope_tables(place, lens):
    chip, core = place // 2, place % 2
    k = jnp.arange(REACH + 1, dtype=i32)[:, None, None]
    half = jnp.arange(2, dtype=i32)[None, :, None]
    t = jnp.arange(TOK, dtype=i32)[None, None, :]
    index = (((chip - k) * 2 + jnp.where(half == 0, core, 1 - core)) * TOK + t).reshape(
        REACH + 1, BLK
    )
    tri = jnp.arange(lens.shape[1])
    ends = jnp.sum(jnp.where(tri[None, :] <= tri[:, None], lens[0][None, :], 0), axis=1)
    start = jnp.max(jnp.where(index[..., None] >= ends, ends, 0), axis=-1)
    freqs = jnp.power(1000000.0, -(jnp.arange(HD // 2, dtype=f32) * (2.0 / HD)))
    angles = (index - start).astype(f32)[..., None] * freqs
    cosine, sine = jnp.cos(angles), jnp.sin(angles)
    return (
        jnp.concatenate([cosine, cosine], axis=-1),
        jnp.concatenate([-sine, sine], axis=-1),
    )


def swap_cores(x):
    return lax.ppermute(x, "ctx", [(i, i ^ 1) for i in range(16)])


def shift_chips(x, k):
    return lax.ppermute(x, "ctx", [(i, i + 2 * k) for i in range(16) if 0 <= i + 2 * k < 16])


def on_device(queries, keys, values, out_grad, q_gain, k_gain, lengths, prompt_ids, grades):
    place = lax.axis_index("ctx")
    core = place % 2
    q_gain2, k_gain2 = q_gain.reshape(1, HD), k_gain.reshape(1, HD)

    kv = jnp.stack([keys, values]).transpose(2, 0, 1, 3).reshape(2, HEADS, 2, TOK, HD)
    kv = kv.transpose(0, 2, 1, 3, 4)
    kv_mine = lax.dynamic_index_in_dim(kv, core, 0, keepdims=False)
    kv_other = swap_cores(lax.dynamic_index_in_dim(kv, 1 - core, 0, keepdims=False))
    own = jnp.stack([kv_mine, kv_other])
    blocks = [own] + [shift_chips(own, k) for k in range(1, REACH + 1)]

    heads = HEADS * GROUP
    q_t = queries.transpose(1, 0, 2).reshape(2, heads, TOK, HD)
    g_t = out_grad.transpose(1, 0, 2).reshape(2, heads, TOK, HD)
    q_other = swap_cores(lax.dynamic_index_in_dim(q_t, 1 - core, 0, keepdims=False))
    g_other = swap_cores(lax.dynamic_index_in_dim(g_t, 1 - core, 0, keepdims=False))
    cosine, sine = rope_tables(place, lengths)

    rows = jax.ShapeDtypeStruct((SLOTS, BLK, HD), bf16)
    q, g = pl.pallas_call(
        prep_kernel,
        out_shape=[rows, rows],
        in_specs=smem(3) + vmem(9),
        out_specs=vmem(2),
        compiler_params=VMEM,
        name="prepare",
    )(
        lengths, prompt_ids, grades, prompt_ids, grades,
        q_t, q_other, g_t, g_other, q_gain2, cosine, sine,
    )

    common = (lengths, k_gain2, cosine, sine, q, g)
    state = forward((0,), *common, blocks[:1], None)
    state = forward((1, 2, 3, 4), *common, blocks[1:], state)
    dq, terms, pack4, pack3 = backward((4, 3), *common, state, [blocks[4], blocks[3]], None, None)
    back4, back3 = shift_chips(pack4, -4), shift_chips(pack3, -3)
    dq, terms, pack2, pack1 = backward(
        (2, 1), *common, state, [blocks[2], blocks[1]], (dq, terms), None
    )
    back2, back1 = shift_chips(pack2, -2), shift_chips(pack1, -1)
    q_half, terms, dk, dv = backward(
        (0,), *common, state, blocks[:1], (dq, terms), (q_t, q_other, q_gain2)
    )

    q_swapped = swap_cores(q_half[1])
    first = jnp.where(core == 0, q_half[0], q_swapped)
    second = jnp.where(core == 0, q_swapped, q_half[0])
    q_grad = jnp.concatenate([first, second]).transpose(1, 0, 2)

    pair = terms[:2].reshape(1, 2 * HD)
    count = lax.axis_size("dp") * lax.axis_size("ctx")
    gathered = lax.all_to_all(
        jnp.broadcast_to(pair, (count, 2 * HD)), ("dp", "ctx"), 0, 0, tiled=True
    )
    gains = jnp.sum(gathered, axis=0)

    out = pl.pallas_call(
        finish_kernel,
        out_shape=jax.ShapeDtypeStruct((2, 2, HEADS, TOK, HD), bf16),
        in_specs=vmem(10),
        out_specs=vmem(1)[0],
        compiler_params=VMEM,
        name="finish",
    )(k_gain2, cosine, sine, own, dk, dv, back1, back2, back3, back4)
    mine, other = out[0], swap_cores(out[1])
    first = jnp.where(core == 0, mine, other)
    second = jnp.where(core == 0, other, mine)
    kv_grad = jnp.concatenate([first, second], axis=1).transpose(0, 2, 1, 3)
    return (q_grad, kv_grad[0], kv_grad[1], gains[:HD], gains[HD:])


def solution(mesh):
    rows = P(("dp", "ctx"), None, None)
    return jax.shard_map(
        on_device,
        mesh=mesh,
        in_specs=(rows, rows, rows, rows, P(), P(), P("dp", None), P(), P()),
        out_specs=(rows, rows, rows, P(), P()),
        check_vma=False,
    )
```

```python
import functools
import math

import jax
import jax.numpy as jnp
from jax import lax
from jax.experimental import pallas as pl
from jax.experimental.pallas import tpu as pltpu
from jax.sharding import PartitionSpec as P

EPS = 1e-06
TOK = 128
HD = 128
BLK = 2 * TOK
REACH = 4
GROUP = 8
HEADS = 2
SLOTS = HEADS * 2 * (GROUP // 2)
ROOT = 1.0 / math.sqrt(HD)
EXP_SCALE = ROOT * math.log2(math.e)
MASKED = -1e30
UNROLL = 4
QMAX = 32000.0
GAP_MAX = 64.0 / EXP_SCALE
VMEM = pltpu.CompilerParams(vmem_limit_bytes=56 * 1024 * 1024)

f32, bf16, i32 = jnp.float32, jnp.bfloat16, jnp.int32


def dot(a, b, dims):
    return lax.dot_general(a, b, (dims, ((), ())), preferred_element_type=f32)


def inv_rms(x):
    return lax.rsqrt(jnp.mean(x * x, axis=-1, keepdims=True) + EPS)


def turn(x):
    return pltpu.roll(x, HD // 2, x.ndim - 1)


def tables(cs):
    other = turn(cs)
    low = lax.broadcasted_iota(i32, cs.shape, cs.ndim - 1) < HD // 2
    return jnp.where(low, cs, other), jnp.where(low, -other, cs)


def norm_rope(x, gain, cosine, sine):
    xn = x * inv_rms(x) * gain
    return xn * cosine + turn(xn) * sine


def unrotate(x, gain, cosine, sine, incoming):
    dn = incoming * cosine - turn(incoming) * sine
    r = inv_rms(x)
    unit = x * r
    u = dn * gain
    grad = r * (u - unit * jnp.mean(u * unit, axis=-1, keepdims=True))
    return grad, jnp.sum(dn * unit, axis=0, keepdims=True)


def token_base(place, k, half):
    chip, core = place // 2, place % 2
    return ((chip - k) * 2 + jnp.where(half == 0, core, 1 - core)) * TOK


def fill_bias(bias, blocks, half, lens):
    place = lax.axis_index("ctx")
    qidx = token_base(place, 0, half) + lax.broadcasted_iota(i32, (1, TOK), 1)
    start, total = jnp.zeros_like(qidx), jnp.int32(0)
    for j in range(lens.shape[1]):
        total = total + lens[0, j]
        start = jnp.where(qidx >= total, total, start)
    for n, k in enumerate(blocks):
        for part in range(2):
            kidx = token_base(place, k, part) + lax.broadcasted_iota(i32, (TOK, TOK), 0)
            good = (kidx <= qidx) & (kidx >= start)
            at = n * BLK + part * TOK
            bias[half, at : at + TOK, :] = jnp.where(good, 0.0, MASKED)


def load_block(n, k, kv, cs, gain_row, kr, vv):
    for part in range(2):
        rows = slice(part * TOK, (part + 1) * TOK)
        at = n * BLK + part * TOK
        cosine, sine = tables(cs[k, rows, :])
        x = kv[part, 0, 0].astype(f32)
        kr[at : at + TOK, :] = norm_rope(x, gain_row, cosine, sine).astype(bf16)
        vv[at : at + TOK, :] = kv[part, 1, 0]


def widen(ref, rows):
    half = ref[rows, :]
    return jnp.concatenate([half, half], axis=1)


def prep_kernel(
    lens, ids, grades, q_own, q_other, g_own, g_other, q_gain, k_gain, cs, kv,
    q_out, g_out, m_out, l_out, d_out, kr_out, kr, vv, bias, weights,
):
    head, half = pl.program_id(0), pl.program_id(1)
    place, row = lax.axis_index("ctx"), lax.axis_index("dp")

    @pl.when((half == 0) & (head == 0))
    def _():
        adv = []
        pid, grd = ids[...].astype(f32), grades[...].astype(f32)
        at_row = lax.broadcasted_iota(i32, pid.shape, 0) == row
        at_col = lax.broadcasted_iota(i32, pid.shape, 1)
        for j in range(lens.shape[1]):
            at = at_row & (at_col == j)
            name = jnp.sum(jnp.where(at, pid, 0.0), keepdims=True)
            own = jnp.sum(jnp.where(at, grd, 0.0), keepdims=True)
            same = jnp.where(pid == name, 1.0, 0.0)
            count = jnp.sum(same, keepdims=True)
            centre = jnp.sum(same * grd, keepdims=True) / count
            spread = grd - centre
            variance = jnp.sum(same * spread * spread, keepdims=True) / count
            adv.append((own - centre) / jnp.maximum(jnp.sqrt(variance), 1.0))
        for part in range(2):
            idx = token_base(place, 0, part) + lax.broadcasted_iota(i32, (TOK, HD), 0)
            weight = jnp.zeros((TOK, HD), f32)
            total = jnp.int32(0)
            for j in range(lens.shape[1]):
                weight = jnp.where(idx >= total, adv[j], weight)
                total = total + lens[0, j]
            weights[part] = weight
            fill_bias(bias, (0,), part, lens)

    @pl.when(half == 0)
    def _():
        load_block(0, 0, kv, cs, k_gain[...], kr, vv)
        kr_out[0] = kr[...]

    rows = pl.ds(pl.multiple_of(half * TOK, TOK), TOK)
    cosine, sine = tables(cs[0, rows, :])
    first = half == 0

    def body(two, carry):
        for e in range(2):
            n = two * 2 + e
            x = jnp.where(first, q_own[n], q_other[n]).astype(f32)
            g = jnp.where(first, g_own[n], g_other[n]).astype(f32)
            at = slice(e * TOK, (e + 1) * TOK)
            q_out[two, at, :] = norm_rope(x, q_gain[...], cosine, sine).astype(bf16)
            g_out[two, at, :] = (weights[half] * g).astype(bf16)
        s = dot(kr[...], q_out[two], ((1,), (1,))) + widen(bias.at[half], slice(None))
        dp = dot(vv[...], g_out[two], ((1,), (1,)))
        m = jnp.max(s, axis=0, keepdims=True)
        e = jnp.exp2((s - m) * EXP_SCALE)
        m_out[two] = m
        l_out[two] = jnp.sum(e, axis=0, keepdims=True)
        d_out[two] = jnp.sum(e * dp, axis=0, keepdims=True)
        return carry

    lax.fori_loop(0, GROUP // 2, body, 0, unroll=UNROLL)


def gain_term(k, n, kv, cs, dk):
    total = jnp.zeros((1, HD), f32)
    for part in range(2):
        rows = slice(part * TOK, (part + 1) * TOK)
        at = n * BLK + part * TOK
        cosine, sine = tables(cs[k, rows, :])
        x = kv[part, 0, 0].astype(f32)
        incoming = dk[at : at + TOK, :]
        dn = incoming * cosine - turn(incoming) * sine
        total = total + jnp.sum(dn * (x * inv_rms(x)), axis=0, keepdims=True)
    return total * ROOT


def code(n, head, dk, dv, packed):
    marks = packed[2 * HEADS * BLK :, :].astype(i32).astype(f32)
    rows = lax.broadcasted_iota(i32, (16, HD), 0)
    for kind, ref in enumerate((dk, dv)):
        x = ref[n * BLK : (n + 1) * BLK, :]
        peak = jnp.maximum(jnp.max(jnp.abs(x), axis=0, keepdims=True), 1e-30)
        mark = jnp.ceil(jnp.log2(peak) * 256.0)
        marks = jnp.where(rows == kind * HEADS + head, mark, marks)
        fixed = x * (jnp.exp2(mark * (-1.0 / 256.0)) * QMAX)
        at = pl.multiple_of((kind * HEADS + head) * BLK, BLK)
        packed[pl.ds(at, BLK), :] = jnp.floor(fixed + 0.5).astype(i32).astype(jnp.int16)
    packed[2 * HEADS * BLK :, :] = marks.astype(i32).astype(jnp.int16)


FAR = (4, 3, 2, 1)
NEAR = (2, 1, 0)


def far_kernel(
    lens, k_gain, cs, q, g, m_in, l_in, d_in, kv4, kv3, kv2, kv1,
    dq, lse_out, mean_out, terms, pack4, pack3, kr_out, kr, vv, krt, bias, dk, dv,
):
    head, half = pl.program_id(0), pl.program_id(1)
    kvs, packs = (kv4, kv3, kv2, kv1), (pack4, pack3)
    done = len(packs) * BLK
    place = lax.axis_index("ctx")
    base, total, opening = token_base(place, 0, half), jnp.int32(0), jnp.int32(0)
    for j in range(lens.shape[1]):
        total = total + lens[0, j]
        opening = jnp.where(base >= total, total, opening)
    reaches = opening < (place // 2) * BLK

    @pl.when((head == 0) & (half == 0))
    def _():
        terms[...] = jnp.zeros(terms.shape, f32)
        for pack in packs:
            pack[2 * HEADS * BLK :, :] = jnp.zeros((16, HD), jnp.int16)
        for part in range(2):
            fill_bias(bias, FAR, part, lens)

    @pl.when(half == 0)
    def _():
        for n, k in enumerate(FAR):
            load_block(n, k, kvs[n], cs, k_gain[...], kr, vv)
        krt[...] = jnp.transpose(kr[:done, :].astype(f32)).astype(bf16)
        kr_out[0] = kr[done:, :]

    dk[half] = jnp.zeros(dk.shape[1:], f32)
    dv[half] = jnp.zeros(dv.shape[1:], f32)

    def finish(two, e, dp, m, l, d):
        mean = d / l
        lse_out[two] = m * EXP_SCALE + jnp.log2(l)
        mean_out[two] = mean
        p = e[:done] * (1.0 / l)
        ds = (p * (dp[:done] - mean)).astype(bf16)
        dv[half] += dot(p.astype(bf16), g[two], ((1,), (0,)))
        dk[half] += dot(ds, q[two], ((1,), (0,)))
        dq[two] = dot(krt[...], ds, ((1,), (0,)))

    def products(two):
        s = dot(kr[...], q[two], ((1,), (1,))) + widen(bias.at[half], slice(None))
        return s, dot(vv[...], g[two], ((1,), (1,)))

    def near_peak(two, above):
        s, dp = products(two)
        m = m_in[two]
        gap = s - m
        e = jnp.exp2(gap * EXP_SCALE)
        l = l_in[two] + jnp.sum(e, axis=0, keepdims=True)
        d = d_in[two] + jnp.sum(e * dp, axis=0, keepdims=True)
        finish(two, e, dp, m, l, d)
        return jnp.maximum(above, jnp.max(gap, axis=0, keepdims=True))

    def any_peak(two, carry):
        s, dp = products(two)
        m_old = m_in[two]
        m = jnp.maximum(m_old, jnp.max(s, axis=0, keepdims=True))
        e = jnp.exp2((s - m) * EXP_SCALE)
        fade = jnp.exp2((m_old - m) * EXP_SCALE)
        l = l_in[two] * fade + jnp.sum(e, axis=0, keepdims=True)
        d = d_in[two] * fade + jnp.sum(e * dp, axis=0, keepdims=True)
        finish(two, e, dp, m, l, d)
        return carry

    @pl.when(reaches)
    def _():
        start = jnp.full((1, BLK), MASKED, f32)
        above = lax.fori_loop(0, GROUP // 2, near_peak, start, unroll=UNROLL)

        @pl.when(jnp.max(above) > GAP_MAX)
        def _():
            dk[half] = jnp.zeros(dk.shape[1:], f32)
            dv[half] = jnp.zeros(dv.shape[1:], f32)
            lax.fori_loop(0, GROUP // 2, any_peak, 0)

    @pl.when(jnp.logical_not(reaches))
    def _():
        lse_out[...] = m_in[...] * EXP_SCALE + jnp.log2(l_in[...])
        mean_out[...] = d_in[...] / l_in[...]
        dq[...] = jnp.zeros(dq.shape, f32)

    @pl.when(half == 1)
    def _():
        dk[0] += dk[1]
        dv[0] += dv[1]
        for n, k in enumerate(FAR[: len(packs)]):
            terms[1:2, :] = terms[1:2, :] + gain_term(k, n, kvs[n], cs, dk.at[0])
            code(n, head, dk.at[0], dv.at[0], packs[n])


def near_kernel(
    lens, q_gain, cs, q, g, lse, mean, dq_in, terms_in, q_own, q_other, kr21, kr0, kv2, kv1, kv0,
    q_grad, terms, pack2, pack1, dk_own, dv_own, kr, vv, krt, bias, dk, dv,
):
    head, half = pl.program_id(0), pl.program_id(1)
    kvs, packs = (kv2, kv1, kv0), (pack2, pack1)

    @pl.when((head == 0) & (half == 0))
    def _():
        terms[...] = terms_in[...]
        for pack in packs:
            pack[2 * HEADS * BLK :, :] = jnp.zeros((16, HD), jnp.int16)
        for part in range(2):
            fill_bias(bias, NEAR, part, lens)

    @pl.when(half == 0)
    def _():
        kr[: 2 * BLK, :] = kr21[0]
        kr[2 * BLK :, :] = kr0[0]
        for n in range(len(NEAR)):
            for part in range(2):
                at = n * BLK + part * TOK
                vv[at : at + TOK, :] = kvs[n][part, 1, 0]
        krt[...] = jnp.transpose(kr[...].astype(f32)).astype(bf16)
        dk[...] = jnp.zeros(dk.shape, f32)
        dv[...] = jnp.zeros(dv.shape, f32)

    rows = pl.ds(pl.multiple_of(half * TOK, TOK), TOK)
    cosine, sine = tables(cs[0, rows, :])
    first = half == 0

    def body(two, total):
        s = dot(kr[...], q[two], ((1,), (1,))) + widen(bias.at[half], slice(None))
        dp = dot(vv[...], g[two], ((1,), (1,)))
        p = jnp.exp2(s * EXP_SCALE - lse[two])
        ds = (p * (dp - mean[two])).astype(bf16)
        dv[...] += dot(p.astype(bf16), g[two], ((1,), (0,)))
        dk[...] += dot(ds, q[two], ((1,), (0,)))
        incoming = jnp.transpose(dq_in[two] + dot(krt[...], ds, ((1,), (0,)))) * ROOT
        for e in range(2):
            n = two * 2 + e
            x = jnp.where(first, q_own[n], q_other[n]).astype(f32)
            grad, part = unrotate(
                x, q_gain[...], cosine, sine, incoming[e * TOK : (e + 1) * TOK, :]
            )
            q_grad[0, n] = grad.astype(bf16)
            total = total + part
        return total

    total = lax.fori_loop(0, GROUP // 2, body, jnp.zeros((1, HD), f32), unroll=UNROLL)
    terms[0:1, :] = terms[0:1, :] + total

    @pl.when(half == 1)
    def _():
        for n, k in enumerate(NEAR):
            terms[1:2, :] = terms[1:2, :] + gain_term(k, n, kvs[n], cs, dk)
            if k > 0:
                code(n, head, dk, dv, packs[n])
            else:
                dk_own[0] = dk[n * BLK : (n + 1) * BLK, :]
                dv_own[0] = dv[n * BLK : (n + 1) * BLK, :]


def finish_kernel(gain, cs, kv, dk, dv, p1, p2, p3, p4, mine, other):
    gain_row = gain[...]
    packs, outs = (p1, p2, p3, p4), (mine, other)
    marks = [p[2 * HEADS * BLK :, :].astype(i32).astype(f32) for p in packs]
    for kind, ref in enumerate((dk, dv)):
        for head in range(HEADS):
            n = kind * HEADS + head
            scales = [jnp.exp2(k[n : n + 1, :] * (1.0 / 256.0)) * (1.0 / QMAX) for k in marks]
            for half in range(2):
                rows = slice(half * TOK, (half + 1) * TOK)
                total = ref[head, rows, :]
                for p, scale in zip(packs, scales):
                    at = n * BLK + half * TOK
                    total = total + p[at : at + TOK, :].astype(i32).astype(f32) * scale
                if kind == 0:
                    x = kv[half, 0, head].astype(f32)
                    cosine, sine = tables(cs[0, rows, :])
                    total, _ = unrotate(x, gain_row, cosine, sine, total * ROOT)
                outs[half][kind, head] = total.astype(bf16)


def vmem(count):
    return [pl.BlockSpec(memory_space=pltpu.VMEM)] * count


def smem(count):
    return [pl.BlockSpec(memory_space=pltpu.SMEM)] * count


def spec(shape, index):
    return pl.BlockSpec(shape, index)


PAIRS = GROUP // 2
Q_BLOCK = (PAIRS, BLK, HD)
STAT_BLOCK = (PAIRS, 1, BLK)
DQ_BLOCK = (PAIRS, HD, BLK)
RAW_BLOCK = (GROUP, TOK, HD)
KV_BLOCK = (2, 2, 1, TOK, HD)
STAT = jax.ShapeDtypeStruct((SLOTS, 1, BLK), f32)
TERMS = jax.ShapeDtypeStruct((8, HD), f32)
PACK = jax.ShapeDtypeStruct((2 * HEADS * BLK + 16, HD), jnp.int16)
OWN = jax.ShapeDtypeStruct((HEADS, BLK, HD), f32)


def by_slot(head, half):
    return (head * 2 + half, 0, 0)


def by_head(head, half):
    return (head, 0, 0)


def kv_at(head, half):
    return (0, 0, head, 0, 0)


def whole(ndim):
    return lambda head, half: (0,) * ndim


def own_raw(head, half):
    return (head, 0, 0)


def block_scratch(done, blocks):
    return [
        pltpu.VMEM((blocks * BLK, HD), bf16),
        pltpu.VMEM((blocks * BLK, HD), bf16),
        pltpu.VMEM((HD, done * BLK), bf16),
        pltpu.VMEM((2, blocks * BLK, TOK), f32),
        pltpu.VMEM((done * BLK, HD), f32),
        pltpu.VMEM((done * BLK, HD), f32),
    ]


def prepare(lengths, ids, grades, q_own, q_other, g_own, g_other, q_gain, k_gain, cs, kv):
    rows = jax.ShapeDtypeStruct((SLOTS, BLK, HD), bf16)
    return pl.pallas_call(
        prep_kernel,
        grid=(HEADS, 2),
        out_shape=[rows, rows, STAT, STAT, STAT, jax.ShapeDtypeStruct((HEADS, BLK, HD), bf16)],
        in_specs=smem(1)
        + [spec(ids.shape, whole(2))] * 2
        + [spec(RAW_BLOCK, own_raw)] * 4
        + [spec((1, HD), whole(2))] * 2
        + [spec((1, BLK, HD), whole(3)), spec(KV_BLOCK, kv_at)],
        out_specs=[spec(Q_BLOCK, by_slot)] * 2
        + [spec(STAT_BLOCK, by_slot)] * 3
        + [spec((1, BLK, HD), by_head)],
        scratch_shapes=[
            pltpu.VMEM((BLK, HD), bf16),
            pltpu.VMEM((BLK, HD), bf16),
            pltpu.VMEM((2, BLK, TOK), f32),
            pltpu.VMEM((2, TOK, HD), f32),
        ],
        compiler_params=VMEM,
        name="prepare",
    )(lengths, ids, grades, q_own, q_other, g_own, g_other, q_gain, k_gain, cs, kv)


def far(lengths, k_gain, cs, q, g, stats, kvs):
    dq = jax.ShapeDtypeStruct((SLOTS, HD, BLK), f32)
    near_keys = jax.ShapeDtypeStruct((HEADS, 2 * BLK, HD), bf16)
    return pl.pallas_call(
        far_kernel,
        grid=(HEADS, 2),
        out_shape=[dq, STAT, STAT, TERMS, PACK, PACK, near_keys],
        in_specs=smem(1)
        + [spec((1, HD), whole(2)), spec(cs.shape, whole(3))]
        + [spec(Q_BLOCK, by_slot)] * 2
        + [spec(STAT_BLOCK, by_slot)] * 3
        + [spec(KV_BLOCK, kv_at)] * 4,
        out_specs=[spec(DQ_BLOCK, by_slot), spec(STAT_BLOCK, by_slot), spec(STAT_BLOCK, by_slot)]
        + [spec(TERMS.shape, whole(2))]
        + [spec(PACK.shape, whole(2))] * 2
        + [spec((1, 2 * BLK, HD), by_head)],
        scratch_shapes=block_scratch(2, 4)[:4] + [pltpu.VMEM((2, 2 * BLK, HD), f32)] * 2,
        compiler_params=VMEM,
        name="far",
    )(lengths, k_gain, cs, q, g, *stats, *kvs)


def near(lengths, q_gain, cs, q, g, lse, mean, dq, terms, q_own, q_other, kr21, kr0, kvs):
    row = spec((1, HD), whole(2))
    return pl.pallas_call(
        near_kernel,
        grid=(HEADS, 2),
        out_shape=[
            jax.ShapeDtypeStruct((2, HEADS * GROUP, TOK, HD), bf16),
            TERMS, PACK, PACK, OWN, OWN,
        ],
        in_specs=smem(1)
        + [row, spec((3, BLK, HD), whole(3))]
        + [spec(Q_BLOCK, by_slot)] * 2
        + [spec(STAT_BLOCK, by_slot)] * 2
        + [spec(DQ_BLOCK, by_slot), spec(TERMS.shape, whole(2))]
        + [spec(RAW_BLOCK, own_raw)] * 2
        + [spec((1, 2 * BLK, HD), by_head), spec((1, BLK, HD), by_head)]
        + [spec(KV_BLOCK, kv_at)] * 3,
        out_specs=[spec((1,) + RAW_BLOCK, lambda head, half: (half, head, 0, 0))]
        + [spec(TERMS.shape, whole(2))]
        + [spec(PACK.shape, whole(2))] * 2
        + [spec((1, BLK, HD), by_head)] * 2,
        scratch_shapes=block_scratch(3, 3),
        compiler_params=VMEM,
        name="near",
    )(lengths, q_gain, cs, q, g, lse, mean, dq, terms, q_own, q_other, kr21, kr0, *kvs)


def rope_tables(place, lens):
    chip, core = place // 2, place % 2
    k = jnp.arange(REACH + 1, dtype=i32)[:, None, None]
    half = jnp.arange(2, dtype=i32)[None, :, None]
    t = jnp.arange(TOK, dtype=i32)[None, None, :]
    index = (((chip - k) * 2 + jnp.where(half == 0, core, 1 - core)) * TOK + t).reshape(
        REACH + 1, BLK
    )
    tri = jnp.arange(lens.shape[1])
    ends = jnp.sum(jnp.where(tri[None, :] <= tri[:, None], lens[0][None, :], 0), axis=1)
    start = jnp.max(jnp.where(index[..., None] >= ends, ends, 0), axis=-1)
    freqs = jnp.power(1000000.0, -(jnp.arange(HD // 2, dtype=f32) * (2.0 / HD)))
    angles = (index - start).astype(f32)[..., None] * freqs
    return jnp.concatenate([jnp.cos(angles), jnp.sin(angles)], axis=-1)


def swap_cores(x):
    return lax.ppermute(x, "ctx", [(i, i ^ 1) for i in range(16)])


def shift_chips(x, k):
    return lax.ppermute(x, "ctx", [(i, i + 2 * k) for i in range(16) if 0 <= i + 2 * k < 16])


def on_device(queries, keys, values, out_grad, q_gain, k_gain, lengths, prompt_ids, grades):
    place = lax.axis_index("ctx")
    core = place % 2
    q_gain2, k_gain2 = q_gain.reshape(1, HD), k_gain.reshape(1, HD)

    kv = jnp.stack([keys, values]).transpose(2, 0, 1, 3).reshape(2, HEADS, 2, TOK, HD)
    kv = kv.transpose(0, 2, 1, 3, 4)
    kv_mine = lax.dynamic_index_in_dim(kv, core, 0, keepdims=False)
    kv_other = swap_cores(lax.dynamic_index_in_dim(kv, 1 - core, 0, keepdims=False))
    own = jnp.stack([kv_mine, kv_other])
    blocks = [own] + [shift_chips(own, k) for k in range(1, REACH + 1)]

    heads = HEADS * GROUP
    q_t = queries.transpose(1, 0, 2).reshape(2, heads, TOK, HD)
    g_t = out_grad.transpose(1, 0, 2).reshape(2, heads, TOK, HD)
    q_own = lax.dynamic_index_in_dim(q_t, core, 0, keepdims=False)
    g_own = lax.dynamic_index_in_dim(g_t, core, 0, keepdims=False)
    q_other = swap_cores(lax.dynamic_index_in_dim(q_t, 1 - core, 0, keepdims=False))
    g_other = swap_cores(lax.dynamic_index_in_dim(g_t, 1 - core, 0, keepdims=False))
    cs = rope_tables(place, lengths)

    q, g, m, l, d, kr0 = prepare(
        lengths, prompt_ids, grades, q_own, q_other, g_own, g_other, q_gain2, k_gain2, cs, own
    )
    dq, lse, mean, terms, pack4, pack3, kr21 = far(
        lengths, k_gain2, cs, q, g, (m, l, d), [blocks[k] for k in FAR]
    )
    back4, back3 = shift_chips(pack4, -4), shift_chips(pack3, -3)
    q_half, terms, pack2, pack1, dk, dv = near(
        lengths, q_gain2, cs, q, g, lse, mean, dq, terms, q_own, q_other, kr21, kr0,
        [blocks[k] for k in NEAR],
    )
    back2, back1 = shift_chips(pack2, -2), shift_chips(pack1, -1)

    q_swapped = swap_cores(q_half[1])
    first = jnp.where(core == 0, q_half[0], q_swapped)
    second = jnp.where(core == 0, q_swapped, q_half[0])
    q_grad = jnp.concatenate([first, second]).transpose(1, 0, 2)

    pair = terms[:2].reshape(1, 2 * HD)
    pair, back4, back3 = lax.optimization_barrier((pair, back4, back3))
    count = lax.axis_size("dp") * lax.axis_size("ctx")
    gathered = lax.all_to_all(
        jnp.broadcast_to(pair, (count, 2 * HD)), ("dp", "ctx"), 0, 0, tiled=True
    )
    gains = jnp.sum(gathered, axis=0)

    mine, other = pl.pallas_call(
        finish_kernel,
        out_shape=[jax.ShapeDtypeStruct((2, HEADS, TOK, HD), bf16)] * 2,
        in_specs=vmem(9),
        out_specs=vmem(2),
        compiler_params=VMEM,
        name="finish",
    )(k_gain2, cs, own, dk, dv, back1, back2, back3, back4)
    other = swap_cores(other)
    first = jnp.where(core == 0, mine, other)
    second = jnp.where(core == 0, other, mine)
    kv_grad = jnp.concatenate([first, second], axis=1).transpose(0, 2, 1, 3)
    return (q_grad, kv_grad[0], kv_grad[1], gains[:HD], gains[HD:])


def solution(mesh):
    rows = P(("dp", "ctx"), None, None)
    return jax.shard_map(
        on_device,
        mesh=mesh,
        in_specs=(rows, rows, rows, rows, P(), P(), P("dp", None), P(), P()),
        out_specs=(rows, rows, rows, P(), P()),
        check_vma=False,
    )
```

```python
import functools
import math

import jax
import jax.numpy as jnp
from jax import lax
from jax.experimental import pallas as pl
from jax.experimental.pallas import tpu as pltpu
from jax.sharding import PartitionSpec as P

EPS = 1e-06
TOK = 128
HD = 128
BLK = 2 * TOK
REACH = 4
GROUP = 8
HEADS = 2
SLOTS = HEADS * 2 * (GROUP // 2)
ROOT = 1.0 / math.sqrt(HD)
EXP_SCALE = ROOT * math.log2(math.e)
MASKED = -1e30
UNROLL = 4
QMAX = 32000.0
GAP_MAX = 64.0 / EXP_SCALE
VMEM = pltpu.CompilerParams(vmem_limit_bytes=56 * 1024 * 1024)

f32, bf16, i32 = jnp.float32, jnp.bfloat16, jnp.int32


def dot(a, b, dims):
    return lax.dot_general(a, b, (dims, ((), ())), preferred_element_type=f32)


def inv_rms(x):
    return lax.rsqrt(jnp.mean(x * x, axis=-1, keepdims=True) + EPS)


def inv_rms_wide(x):
    ones = jnp.full((HD, HD), 1.0 / HD, bf16)
    square = x * x
    high = square.astype(bf16)
    low = (square - high.astype(f32)).astype(bf16)
    return lax.rsqrt(dot(high, ones, ((1,), (0,))) + dot(low, ones, ((1,), (0,))) + EPS)


def turn(x):
    return pltpu.roll(x, HD // 2, x.ndim - 1)


def tables(cs):
    other = turn(cs)
    low = lax.broadcasted_iota(i32, cs.shape, cs.ndim - 1) < HD // 2
    return jnp.where(low, cs, other), jnp.where(low, -other, cs)


def norm_rope(x, r, gain, cosine, sine):
    xn = x * r * gain
    return xn * cosine + turn(xn) * sine


def unrotate(x, gain, cosine, sine, incoming):
    dn = incoming * cosine - turn(incoming) * sine
    r = inv_rms(x)
    unit = x * r
    u = dn * gain
    grad = r * (u - unit * jnp.mean(u * unit, axis=-1, keepdims=True))
    return grad, jnp.sum(dn * unit, axis=0, keepdims=True)


def token_base(place, k, half):
    chip, core = place // 2, place % 2
    return ((chip - k) * 2 + jnp.where(half == 0, core, 1 - core)) * TOK


def fill_bias(bias, blocks, half, lens):
    place = lax.axis_index("ctx")
    qidx = token_base(place, 0, half) + lax.broadcasted_iota(i32, (1, TOK), 1)
    start, total = jnp.zeros_like(qidx), jnp.int32(0)
    for j in range(lens.shape[1]):
        total = total + lens[0, j]
        start = jnp.where(qidx >= total, total, start)
    for n, k in enumerate(blocks):
        for part in range(2):
            kidx = token_base(place, k, part) + lax.broadcasted_iota(i32, (TOK, TOK), 0)
            good = (kidx <= qidx) & (kidx >= start)
            at = n * BLK + part * TOK
            bias[half, at : at + TOK, :] = jnp.where(good, 0.0, MASKED)


def load_block(n, k, kv, cs, gain_row, kr, vv):
    for part in range(2):
        rows = slice(part * TOK, (part + 1) * TOK)
        at = n * BLK + part * TOK
        cosine, sine = tables(cs[k, rows, :])
        x = kv[part, 0, 0].astype(f32)
        kr[at : at + TOK, :] = norm_rope(x, inv_rms_wide(x), gain_row, cosine, sine).astype(bf16)
        vv[at : at + TOK, :] = kv[part, 1, 0]


def widen(ref, rows):
    half = ref[rows, :]
    return jnp.concatenate([half, half], axis=1)


def prep_kernel(
    lens, meta, q_own, q_other, g_own, g_other, q_gain, k_gain, cs, kv,
    q_out, g_out, m_out, l_out, d_out, kr_out, kr, vv, bias, weights,
):
    head, half = pl.program_id(0), pl.program_id(1)
    place, row = lax.axis_index("ctx"), lax.axis_index("dp")

    @pl.when((half == 0) & (head == 0))
    def _():
        count = meta.shape[1]
        ids = jnp.broadcast_to(meta[0:1, :], (count, count))
        same = jnp.where(ids == jnp.transpose(ids), 1.0, 0.0)
        graded = meta[1:2, :]
        column = jnp.transpose(jnp.broadcast_to(graded, (count, count)))
        counted = jnp.sum(same, axis=0, keepdims=True)
        centre = jnp.sum(same * column, axis=0, keepdims=True) / counted
        spread = column - centre
        variance = jnp.sum(same * spread * spread, axis=0, keepdims=True) / counted
        every = (graded - centre) / jnp.maximum(jnp.sqrt(variance), 1.0)
        lane = lax.broadcasted_iota(i32, every.shape, 1) - row * lens.shape[1]
        adv = [
            jnp.sum(jnp.where(lane == j, every, 0.0), keepdims=True) for j in range(lens.shape[1])
        ]
        for part in range(2):
            idx = token_base(place, 0, part) + lax.broadcasted_iota(i32, (TOK, HD), 0)
            weight = jnp.zeros((TOK, HD), f32)
            total = jnp.int32(0)
            for j in range(lens.shape[1]):
                weight = jnp.where(idx >= total, adv[j], weight)
                total = total + lens[0, j]
            weights[part] = weight
            fill_bias(bias, (0,), part, lens)

    @pl.when(half == 0)
    def _():
        load_block(0, 0, kv, cs, k_gain[...], kr, vv)
        kr_out[0] = kr[...]

    rows = pl.ds(pl.multiple_of(half * TOK, TOK), TOK)
    cosine, sine = tables(cs[0, rows, :])
    first = half == 0

    def body(two, carry):
        for e in range(2):
            n = two * 2 + e
            x = jnp.where(first, q_own[n], q_other[n]).astype(f32)
            g = jnp.where(first, g_own[n], g_other[n]).astype(f32)
            at = slice(e * TOK, (e + 1) * TOK)
            q_out[two, at, :] = norm_rope(x, inv_rms(x), q_gain[...], cosine, sine).astype(bf16)
            g_out[two, at, :] = (weights[half] * g).astype(bf16)
        s = dot(kr[...], q_out[two], ((1,), (1,))) + widen(bias.at[half], slice(None))
        dp = dot(vv[...], g_out[two], ((1,), (1,)))
        m = jnp.max(s, axis=0, keepdims=True)
        e = jnp.exp2((s - m) * EXP_SCALE)
        m_out[two] = m
        l_out[two] = jnp.sum(e, axis=0, keepdims=True)
        d_out[two] = jnp.sum(e * dp, axis=0, keepdims=True)
        return carry

    lax.fori_loop(0, GROUP // 2, body, 0, unroll=UNROLL)


def gain_term(k, n, kv, cs, dk):
    total = jnp.zeros((1, HD), f32)
    for part in range(2):
        rows = slice(part * TOK, (part + 1) * TOK)
        at = n * BLK + part * TOK
        cosine, sine = tables(cs[k, rows, :])
        x = kv[part, 0, 0].astype(f32)
        incoming = dk[at : at + TOK, :]
        dn = incoming * cosine - turn(incoming) * sine
        total = total + jnp.sum(dn * (x * inv_rms_wide(x)), axis=0, keepdims=True)
    return total * ROOT


def code(n, head, dk, dv, packed):
    marks = packed[2 * HEADS * BLK :, :].astype(i32).astype(f32)
    rows = lax.broadcasted_iota(i32, (16, HD), 0)
    for kind, ref in enumerate((dk, dv)):
        x = ref[n * BLK : (n + 1) * BLK, :]
        peak = jnp.maximum(jnp.max(jnp.abs(x), axis=0, keepdims=True), 1e-30)
        mark = jnp.ceil(jnp.log2(peak) * 256.0)
        marks = jnp.where(rows == kind * HEADS + head, mark, marks)
        fixed = x * (jnp.exp2(mark * (-1.0 / 256.0)) * QMAX)
        at = pl.multiple_of((kind * HEADS + head) * BLK, BLK)
        packed[pl.ds(at, BLK), :] = jnp.floor(fixed + 0.5).astype(i32).astype(jnp.int16)
    packed[2 * HEADS * BLK :, :] = marks.astype(i32).astype(jnp.int16)


FAR = (4, 3, 2, 1)
NEAR = (2, 1, 0)


def far_kernel(
    lens, k_gain, cs, q, g, m_in, l_in, d_in, kv4, kv3, kv2, kv1,
    dq, lse_out, mean_out, terms, pack4, pack3, kr_out, kr, vv, krt, bias, dk, dv,
):
    head, half = pl.program_id(0), pl.program_id(1)
    kvs, packs = (kv4, kv3, kv2, kv1), (pack4, pack3)
    done = len(packs) * BLK
    place = lax.axis_index("ctx")
    base, total, opening = token_base(place, 0, half), jnp.int32(0), jnp.int32(0)
    for j in range(lens.shape[1]):
        total = total + lens[0, j]
        opening = jnp.where(base >= total, total, opening)
    reaches = opening < (place // 2) * BLK

    @pl.when((head == 0) & (half == 0))
    def _():
        terms[...] = jnp.zeros(terms.shape, f32)
        for pack in packs:
            pack[2 * HEADS * BLK :, :] = jnp.zeros((16, HD), jnp.int16)
        for part in range(2):
            fill_bias(bias, FAR, part, lens)

    @pl.when(half == 0)
    def _():
        for n, k in enumerate(FAR):
            load_block(n, k, kvs[n], cs, k_gain[...], kr, vv)
        krt[...] = jnp.transpose(kr[:done, :].astype(f32)).astype(bf16)
        kr_out[0] = kr[done:, :]

    dk[half] = jnp.zeros(dk.shape[1:], f32)
    dv[half] = jnp.zeros(dv.shape[1:], f32)

    def finish(two, e, dp, m, l, d):
        mean = d / l
        lse_out[two] = m * EXP_SCALE + jnp.log2(l)
        mean_out[two] = mean
        p = e[:done] * (1.0 / l)
        ds = (p * (dp[:done] - mean)).astype(bf16)
        dv[half] += dot(p.astype(bf16), g[two], ((1,), (0,)))
        dk[half] += dot(ds, q[two], ((1,), (0,)))
        dq[two] = dot(krt[...], ds, ((1,), (0,)))

    def products(two):
        s = dot(kr[...], q[two], ((1,), (1,))) + widen(bias.at[half], slice(None))
        return s, dot(vv[...], g[two], ((1,), (1,)))

    def near_peak(two, above):
        s, dp = products(two)
        m = m_in[two]
        gap = s - m
        e = jnp.exp2(gap * EXP_SCALE)
        l = l_in[two] + jnp.sum(e, axis=0, keepdims=True)
        d = d_in[two] + jnp.sum(e * dp, axis=0, keepdims=True)
        finish(two, e, dp, m, l, d)
        return jnp.maximum(above, jnp.max(gap, axis=0, keepdims=True))

    def any_peak(two, carry):
        s, dp = products(two)
        m_old = m_in[two]
        m = jnp.maximum(m_old, jnp.max(s, axis=0, keepdims=True))
        e = jnp.exp2((s - m) * EXP_SCALE)
        fade = jnp.exp2((m_old - m) * EXP_SCALE)
        l = l_in[two] * fade + jnp.sum(e, axis=0, keepdims=True)
        d = d_in[two] * fade + jnp.sum(e * dp, axis=0, keepdims=True)
        finish(two, e, dp, m, l, d)
        return carry

    @pl.when(reaches)
    def _():
        start = jnp.full((1, BLK), MASKED, f32)
        above = lax.fori_loop(0, GROUP // 2, near_peak, start, unroll=UNROLL)

        @pl.when(jnp.max(above) > GAP_MAX)
        def _():
            dk[half] = jnp.zeros(dk.shape[1:], f32)
            dv[half] = jnp.zeros(dv.shape[1:], f32)
            lax.fori_loop(0, GROUP // 2, any_peak, 0)

    @pl.when(jnp.logical_not(reaches))
    def _():
        lse_out[...] = m_in[...] * EXP_SCALE + jnp.log2(l_in[...])
        mean_out[...] = d_in[...] / l_in[...]
        dq[...] = jnp.zeros(dq.shape, f32)

    @pl.when(half == 1)
    def _():
        dk[0] += dk[1]
        dv[0] += dv[1]
        for n, k in enumerate(FAR[: len(packs)]):
            terms[1:2, :] = terms[1:2, :] + gain_term(k, n, kvs[n], cs, dk.at[0])
            code(n, head, dk.at[0], dv.at[0], packs[n])


def near_kernel(
    lens, q_gain, cs, q, g, lse, mean, dq_in, terms_in, q_own, q_other, kr21, kr0, kv2, kv1, kv0,
    q_grad, terms, pack2, pack1, dk_own, dv_own, kr, vv, krt, bias, dk, dv,
):
    head, half = pl.program_id(0), pl.program_id(1)
    kvs, packs = (kv2, kv1, kv0), (pack2, pack1)

    @pl.when((head == 0) & (half == 0))
    def _():
        terms[...] = terms_in[...]
        for pack in packs:
            pack[2 * HEADS * BLK :, :] = jnp.zeros((16, HD), jnp.int16)
        for part in range(2):
            fill_bias(bias, NEAR, part, lens)

    @pl.when(half == 0)
    def _():
        kr[: 2 * BLK, :] = kr21[0]
        kr[2 * BLK :, :] = kr0[0]
        for n in range(len(NEAR)):
            for part in range(2):
                at = n * BLK + part * TOK
                vv[at : at + TOK, :] = kvs[n][part, 1, 0]
        krt[...] = jnp.transpose(kr[...].astype(f32)).astype(bf16)
        dk[...] = jnp.zeros(dk.shape, f32)
        dv[...] = jnp.zeros(dv.shape, f32)

    rows = pl.ds(pl.multiple_of(half * TOK, TOK), TOK)
    cosine, sine = tables(cs[0, rows, :])
    first = half == 0

    def body(two, total):
        s = dot(kr[...], q[two], ((1,), (1,))) + widen(bias.at[half], slice(None))
        dp = dot(vv[...], g[two], ((1,), (1,)))
        p = jnp.exp2(s * EXP_SCALE - lse[two])
        ds = (p * (dp - mean[two])).astype(bf16)
        dv[...] += dot(p.astype(bf16), g[two], ((1,), (0,)))
        dk[...] += dot(ds, q[two], ((1,), (0,)))
        incoming = jnp.transpose(dq_in[two] + dot(krt[...], ds, ((1,), (0,)))) * ROOT
        for e in range(2):
            n = two * 2 + e
            x = jnp.where(first, q_own[n], q_other[n]).astype(f32)
            grad, part = unrotate(
                x, q_gain[...], cosine, sine, incoming[e * TOK : (e + 1) * TOK, :]
            )
            q_grad[0, n] = grad.astype(bf16)
            total = total + part
        return total

    total = lax.fori_loop(0, GROUP // 2, body, jnp.zeros((1, HD), f32), unroll=UNROLL)
    terms[0:1, :] = terms[0:1, :] + total

    @pl.when(half == 1)
    def _():
        for n, k in enumerate(NEAR):
            terms[1:2, :] = terms[1:2, :] + gain_term(k, n, kvs[n], cs, dk)
            if k > 0:
                code(n, head, dk, dv, packs[n])
            else:
                dk_own[0] = dk[n * BLK : (n + 1) * BLK, :]
                dv_own[0] = dv[n * BLK : (n + 1) * BLK, :]


def finish_kernel(gain, cs, kv, dk, dv, p1, p2, p3, p4, mine, other):
    gain_row = gain[...]
    packs, outs = (p1, p2, p3, p4), (mine, other)
    marks = [p[2 * HEADS * BLK :, :].astype(i32).astype(f32) for p in packs]
    for kind, ref in enumerate((dk, dv)):
        for head in range(HEADS):
            n = kind * HEADS + head
            scales = [jnp.exp2(k[n : n + 1, :] * (1.0 / 256.0)) * (1.0 / QMAX) for k in marks]
            for half in range(2):
                rows = slice(half * TOK, (half + 1) * TOK)
                total = ref[head, rows, :]
                for p, scale in zip(packs, scales):
                    at = n * BLK + half * TOK
                    total = total + p[at : at + TOK, :].astype(i32).astype(f32) * scale
                if kind == 0:
                    x = kv[half, 0, head].astype(f32)
                    cosine, sine = tables(cs[0, rows, :])
                    total, _ = unrotate(x, gain_row, cosine, sine, total * ROOT)
                outs[half][kind, head] = total.astype(bf16)


def vmem(count):
    return [pl.BlockSpec(memory_space=pltpu.VMEM)] * count


def smem(count):
    return [pl.BlockSpec(memory_space=pltpu.SMEM)] * count


def spec(shape, index):
    return pl.BlockSpec(shape, index)


PAIRS = GROUP // 2
Q_BLOCK = (PAIRS, BLK, HD)
STAT_BLOCK = (PAIRS, 1, BLK)
DQ_BLOCK = (PAIRS, HD, BLK)
RAW_BLOCK = (GROUP, TOK, HD)
KV_BLOCK = (2, 2, 1, TOK, HD)
STAT = jax.ShapeDtypeStruct((SLOTS, 1, BLK), f32)
TERMS = jax.ShapeDtypeStruct((8, HD), f32)
PACK = jax.ShapeDtypeStruct((2 * HEADS * BLK + 16, HD), jnp.int16)
OWN = jax.ShapeDtypeStruct((HEADS, BLK, HD), f32)


def by_slot(head, half):
    return (head * 2 + half, 0, 0)


def by_head(head, half):
    return (head, 0, 0)


def kv_at(head, half):
    return (0, 0, head, 0, 0)


def whole(ndim):
    return lambda head, half: (0,) * ndim


def own_raw(head, half):
    return (head, 0, 0)


def core_raw(head, half):
    return (lax.axis_index("ctx") % 2, head, 0, 0)


def block_scratch(done, blocks):
    return [
        pltpu.VMEM((blocks * BLK, HD), bf16),
        pltpu.VMEM((blocks * BLK, HD), bf16),
        pltpu.VMEM((HD, done * BLK), bf16),
        pltpu.VMEM((2, blocks * BLK, TOK), f32),
        pltpu.VMEM((done * BLK, HD), f32),
        pltpu.VMEM((done * BLK, HD), f32),
    ]


def prepare(lengths, meta, q_own, q_other, g_own, g_other, q_gain, k_gain, cs, kv):
    rows = jax.ShapeDtypeStruct((SLOTS, BLK, HD), bf16)
    return pl.pallas_call(
        prep_kernel,
        grid=(HEADS, 2),
        out_shape=[rows, rows, STAT, STAT, STAT, jax.ShapeDtypeStruct((HEADS, BLK, HD), bf16)],
        in_specs=smem(1)
        + [spec(meta.shape, whole(2))]
        + [spec((None,) + RAW_BLOCK, core_raw), spec(RAW_BLOCK, own_raw)] * 2
        + [spec((1, HD), whole(2))] * 2
        + [spec((1, BLK, HD), whole(3)), spec(KV_BLOCK, kv_at)],
        out_specs=[spec(Q_BLOCK, by_slot)] * 2
        + [spec(STAT_BLOCK, by_slot)] * 3
        + [spec((1, BLK, HD), by_head)],
        scratch_shapes=[
            pltpu.VMEM((BLK, HD), bf16),
            pltpu.VMEM((BLK, HD), bf16),
            pltpu.VMEM((2, BLK, TOK), f32),
            pltpu.VMEM((2, TOK, HD), f32),
        ],
        compiler_params=VMEM,
        cost_estimate=pl.CostEstimate(
            flops=12_000_000_000, bytes_accessed=6 << 20, transcendentals=SLOTS * BLK * BLK
        ),
        name="prepare",
    )(lengths, meta, q_own, q_other, g_own, g_other, q_gain, k_gain, cs, kv)


def far(lengths, k_gain, cs, q, g, stats, kvs):
    dq = jax.ShapeDtypeStruct((SLOTS, HD, BLK), f32)
    near_keys = jax.ShapeDtypeStruct((HEADS, 2 * BLK, HD), bf16)
    return pl.pallas_call(
        far_kernel,
        grid=(HEADS, 2),
        out_shape=[dq, STAT, STAT, TERMS, PACK, PACK, near_keys],
        in_specs=smem(1)
        + [spec((1, HD), whole(2)), spec(cs.shape, whole(3))]
        + [spec(Q_BLOCK, by_slot)] * 2
        + [spec(STAT_BLOCK, by_slot)] * 3
        + [spec(KV_BLOCK, kv_at)] * 4,
        out_specs=[spec(DQ_BLOCK, by_slot), spec(STAT_BLOCK, by_slot), spec(STAT_BLOCK, by_slot)]
        + [spec(TERMS.shape, whole(2))]
        + [spec(PACK.shape, whole(2))] * 2
        + [spec((1, 2 * BLK, HD), by_head)],
        scratch_shapes=block_scratch(2, 4)[:4] + [pltpu.VMEM((2, 2 * BLK, HD), f32)] * 2,
        compiler_params=VMEM,
        name="far",
    )(lengths, k_gain, cs, q, g, *stats, *kvs)


def near(lengths, q_gain, cs, q, g, lse, mean, dq, terms, q_own, q_other, kr21, kr0, kvs):
    row = spec((1, HD), whole(2))
    return pl.pallas_call(
        near_kernel,
        grid=(HEADS, 2),
        out_shape=[
            jax.ShapeDtypeStruct((2, HEADS * GROUP, TOK, HD), bf16),
            TERMS, PACK, PACK, OWN, OWN,
        ],
        in_specs=smem(1)
        + [row, spec((3, BLK, HD), whole(3))]
        + [spec(Q_BLOCK, by_slot)] * 2
        + [spec(STAT_BLOCK, by_slot)] * 2
        + [spec(DQ_BLOCK, by_slot), spec(TERMS.shape, whole(2))]
        + [spec((None,) + RAW_BLOCK, core_raw), spec(RAW_BLOCK, own_raw)]
        + [spec((1, 2 * BLK, HD), by_head), spec((1, BLK, HD), by_head)]
        + [spec(KV_BLOCK, kv_at)] * 3,
        out_specs=[spec((1,) + RAW_BLOCK, lambda head, half: (half, head, 0, 0))]
        + [spec(TERMS.shape, whole(2))]
        + [spec(PACK.shape, whole(2))] * 2
        + [spec((1, BLK, HD), by_head)] * 2,
        scratch_shapes=block_scratch(3, 3),
        compiler_params=VMEM,
        cost_estimate=pl.CostEstimate(
            flops=16_000_000_000, bytes_accessed=8 << 20, transcendentals=SLOTS * 3 * BLK * BLK
        ),
        name="near",
    )(lengths, q_gain, cs, q, g, lse, mean, dq, terms, q_own, q_other, kr21, kr0, *kvs)


def rope_tables(place, lens):
    chip, core = place // 2, place % 2
    k = jnp.arange(REACH + 1, dtype=i32)[:, None, None]
    half = jnp.arange(2, dtype=i32)[None, :, None]
    t = jnp.arange(TOK, dtype=i32)[None, None, :]
    index = (((chip - k) * 2 + jnp.where(half == 0, core, 1 - core)) * TOK + t).reshape(
        REACH + 1, BLK
    )
    tri = jnp.arange(lens.shape[1])
    ends = jnp.sum(jnp.where(tri[None, :] <= tri[:, None], lens[0][None, :], 0), axis=1)
    start = jnp.max(jnp.where(index[..., None] >= ends, ends, 0), axis=-1)
    lane = jnp.arange(HD, dtype=i32)
    freqs = jnp.power(1000000.0, -((lane % (HD // 2)).astype(f32) * (2.0 / HD)))
    angles = (index - start).astype(f32)[..., None] * freqs
    return jnp.where(lane < HD // 2, jnp.cos(angles), jnp.sin(angles))


def swap_cores(x):
    return lax.ppermute(x, "ctx", [(i, i ^ 1) for i in range(16)])


def shift_chips(x, k):
    return lax.ppermute(x, "ctx", [(i, i + 2 * k) for i in range(16) if 0 <= i + 2 * k < 16])


def on_device(queries, keys, values, out_grad, q_gain, k_gain, lengths, prompt_ids, grades):
    place = lax.axis_index("ctx")
    core = place % 2
    q_gain2, k_gain2 = q_gain.reshape(1, HD), k_gain.reshape(1, HD)

    kv = jnp.stack([keys, values]).transpose(2, 0, 1, 3).reshape(2, HEADS, 2, TOK, HD)
    kv = kv.transpose(0, 2, 1, 3, 4)
    kv_mine = lax.dynamic_index_in_dim(kv, core, 0, keepdims=False)
    kv_other = swap_cores(lax.dynamic_index_in_dim(kv, 1 - core, 0, keepdims=False))
    own = jnp.stack([kv_mine, kv_other])
    blocks = [own, shift_chips(own, 1), shift_chips(own, 2), None, shift_chips(own, 4)]
    blocks[3] = shift_chips(blocks[1], 2)

    heads = HEADS * GROUP
    q_t = queries.transpose(1, 0, 2).reshape(2, heads, TOK, HD)
    g_t = out_grad.transpose(1, 0, 2).reshape(2, heads, TOK, HD)
    q_other = swap_cores(lax.dynamic_index_in_dim(q_t, 1 - core, 0, keepdims=False))
    g_other = swap_cores(lax.dynamic_index_in_dim(g_t, 1 - core, 0, keepdims=False))
    cs = rope_tables(place, lengths)
    meta = jnp.stack([prompt_ids.reshape(-1), grades.reshape(-1)]).astype(f32)

    q, g, m, l, d, kr0 = prepare(
        lengths, meta, q_t, q_other, g_t, g_other, q_gain2, k_gain2, cs, own
    )
    dq, lse, mean, terms, pack4, pack3, kr21 = far(
        lengths, k_gain2, cs, q, g, (m, l, d), [blocks[k] for k in FAR]
    )
    back4, back3 = shift_chips(pack4, -4), shift_chips(pack3, -3)
    q_half, terms, pack2, pack1, dk, dv = near(
        lengths, q_gain2, cs, q, g, lse, mean, dq, terms, q_t, q_other, kr21, kr0,
        [blocks[k] for k in NEAR],
    )
    back2, back1 = shift_chips(pack2, -2), shift_chips(pack1, -1)

    q_swapped = swap_cores(q_half[1])
    first = jnp.where(core == 0, q_half[0], q_swapped)
    second = jnp.where(core == 0, q_swapped, q_half[0])
    q_grad = jnp.concatenate([first, second]).transpose(1, 0, 2)

    pair = terms[:2].reshape(1, 2 * HD)
    count = lax.axis_size("dp") * lax.axis_size("ctx")
    gathered = lax.all_to_all(
        jnp.broadcast_to(pair, (count, 2 * HD)), ("dp", "ctx"), 0, 0, tiled=True
    )
    gains = jnp.sum(gathered, axis=0)

    mine, other = pl.pallas_call(
        finish_kernel,
        out_shape=[jax.ShapeDtypeStruct((2, HEADS, TOK, HD), bf16)] * 2,
        in_specs=vmem(9),
        out_specs=vmem(2),
        compiler_params=VMEM,
        name="finish",
    )(k_gain2, cs, own, dk, dv, back1, back2, back3, back4)
    other = swap_cores(other)
    first = jnp.where(core == 0, mine, other)
    second = jnp.where(core == 0, other, mine)
    kv_grad = jnp.concatenate([first, second], axis=1).transpose(0, 2, 1, 3)
    return (q_grad, kv_grad[0], kv_grad[1], gains[:HD], gains[HD:])


def solution(mesh):
    rows = P(("dp", "ctx"), None, None)
    return jax.shard_map(
        on_device,
        mesh=mesh,
        in_specs=(rows, rows, rows, rows, P(), P(), P("dp", None), P(), P()),
        out_specs=(rows, rows, rows, P(), P()),
        check_vma=False,
    )
```

```python
import functools
import math

import jax
import jax.numpy as jnp
from jax import lax
from jax.experimental import pallas as pl
from jax.experimental.pallas import tpu as pltpu
from jax.sharding import PartitionSpec as P

EPS = 1e-06
TOK = 128
HD = 128
BLK = 2 * TOK
REACH = 4
GROUP = 8
HEADS = 2
SLOTS = HEADS * 2 * (GROUP // 2)
ROOT = 1.0 / math.sqrt(HD)
EXP_SCALE = ROOT * math.log2(math.e)
MASKED = -1e30
UNROLL = 4
QMAX = 32000.0
GAP_MAX = 64.0 / EXP_SCALE
VMEM = pltpu.CompilerParams(vmem_limit_bytes=24 * 1024 * 1024)

f32, bf16, i32 = jnp.float32, jnp.bfloat16, jnp.int32


def dot(a, b, dims):
    return lax.dot_general(a, b, (dims, ((), ())), preferred_element_type=f32)


def inv_rms(x):
    return lax.rsqrt(jnp.mean(x * x, axis=-1, keepdims=True) + EPS)


def inv_rms_wide(x):
    ones = jnp.full((HD, HD), 1.0 / HD, bf16)
    square = x * x
    high = square.astype(bf16)
    low = (square - high.astype(f32)).astype(bf16)
    return lax.rsqrt(dot(high, ones, ((1,), (0,))) + dot(low, ones, ((1,), (0,))) + EPS)


def turn(x):
    return pltpu.roll(x, HD // 2, x.ndim - 1)


def tables(cs):
    other = turn(cs)
    low = lax.broadcasted_iota(i32, cs.shape, cs.ndim - 1) < HD // 2
    return jnp.where(low, cs, other), jnp.where(low, -other, cs)


def norm_rope(x, r, gain, cosine, sine):
    xn = x * r * gain
    return xn * cosine + turn(xn) * sine


def unrotate(x, gain, cosine, sine, incoming):
    dn = incoming * cosine - turn(incoming) * sine
    r = inv_rms(x)
    unit = x * r
    u = dn * gain
    grad = r * (u - unit * jnp.mean(u * unit, axis=-1, keepdims=True))
    return grad, jnp.sum(dn * unit, axis=0, keepdims=True)


def token_base(place, k, half):
    chip, core = place // 2, place % 2
    return ((chip - k) * 2 + jnp.where(half == 0, core, 1 - core)) * TOK


def fill_bias(bias, blocks, half, lens):
    place = lax.axis_index("ctx")
    qidx = token_base(place, 0, half) + lax.broadcasted_iota(i32, (1, TOK), 1)
    start, total = jnp.zeros_like(qidx), jnp.int32(0)
    for j in range(lens.shape[1]):
        total = total + lens[0, j]
        start = jnp.where(qidx >= total, total, start)
    for n, k in enumerate(blocks):
        for part in range(2):
            kidx = token_base(place, k, part) + lax.broadcasted_iota(i32, (TOK, TOK), 0)
            good = (kidx <= qidx) & (kidx >= start)
            at = n * BLK + part * TOK
            bias[half, at : at + TOK, :] = jnp.where(good, 0.0, MASKED)


def load_block(n, k, kv, cs, gain_row, kr, vv):
    for part in range(2):
        rows = slice(part * TOK, (part + 1) * TOK)
        at = n * BLK + part * TOK
        cosine, sine = tables(cs[k, rows, :])
        x = kv[part, 0, 0].astype(f32)
        kr[at : at + TOK, :] = norm_rope(x, inv_rms_wide(x), gain_row, cosine, sine).astype(bf16)
        vv[at : at + TOK, :] = kv[part, 1, 0]


def widen(ref, rows):
    half = ref[rows, :]
    return jnp.concatenate([half, half], axis=1)


def prep_kernel(
    lens, meta, q_own, q_other, g_own, g_other, q_gain, k_gain, cs, kv,
    q_out, g_out, m_out, l_out, d_out, kr_out, kr, vv, bias, weights,
):
    head, half = pl.program_id(0), pl.program_id(1)
    place, row = lax.axis_index("ctx"), lax.axis_index("dp")

    @pl.when((half == 0) & (head == 0))
    def _():
        count = meta.shape[1]
        ids = jnp.broadcast_to(meta[0:1, :], (count, count))
        same = jnp.where(ids == jnp.transpose(ids), 1.0, 0.0)
        graded = meta[1:2, :]
        column = jnp.transpose(jnp.broadcast_to(graded, (count, count)))
        counted = jnp.sum(same, axis=0, keepdims=True)
        centre = jnp.sum(same * column, axis=0, keepdims=True) / counted
        spread = column - centre
        variance = jnp.sum(same * spread * spread, axis=0, keepdims=True) / counted
        every = (graded - centre) / jnp.maximum(jnp.sqrt(variance), 1.0)
        lane = lax.broadcasted_iota(i32, every.shape, 1) - row * lens.shape[1]
        adv = [
            jnp.sum(jnp.where(lane == j, every, 0.0), keepdims=True) for j in range(lens.shape[1])
        ]
        for part in range(2):
            idx = token_base(place, 0, part) + lax.broadcasted_iota(i32, (TOK, HD), 0)
            weight = jnp.zeros((TOK, HD), f32)
            total = jnp.int32(0)
            for j in range(lens.shape[1]):
                weight = jnp.where(idx >= total, adv[j], weight)
                total = total + lens[0, j]
            weights[part] = weight
            fill_bias(bias, (0,), part, lens)

    @pl.when(half == 0)
    def _():
        load_block(0, 0, kv, cs, k_gain[...], kr, vv)
        kr_out[0] = kr[...]

    rows = pl.ds(pl.multiple_of(half * TOK, TOK), TOK)
    cosine, sine = tables(cs[0, rows, :])
    first = half == 0

    def body(two, carry):
        for e in range(2):
            n = two * 2 + e
            x = jnp.where(first, q_own[n], q_other[n]).astype(f32)
            g = jnp.where(first, g_own[n], g_other[n]).astype(f32)
            at = slice(e * TOK, (e + 1) * TOK)
            q_out[two, at, :] = norm_rope(x, inv_rms(x), q_gain[...], cosine, sine).astype(bf16)
            g_out[two, at, :] = (weights[half] * g).astype(bf16)
        s = dot(kr[...], q_out[two], ((1,), (1,))) + widen(bias.at[half], slice(None))
        dp = dot(vv[...], g_out[two], ((1,), (1,)))
        m = jnp.max(s, axis=0, keepdims=True)
        e = jnp.exp2((s - m) * EXP_SCALE)
        m_out[two] = m
        l_out[two] = jnp.sum(e, axis=0, keepdims=True)
        d_out[two] = jnp.sum(e * dp, axis=0, keepdims=True)
        return carry

    lax.fori_loop(0, GROUP // 2, body, 0, unroll=UNROLL)


def gain_term(k, n, kv, cs, dk):
    total = jnp.zeros((1, HD), f32)
    for part in range(2):
        rows = slice(part * TOK, (part + 1) * TOK)
        at = n * BLK + part * TOK
        cosine, sine = tables(cs[k, rows, :])
        x = kv[part, 0, 0].astype(f32)
        incoming = dk[at : at + TOK, :]
        dn = incoming * cosine - turn(incoming) * sine
        total = total + jnp.sum(dn * (x * inv_rms_wide(x)), axis=0, keepdims=True)
    return total * ROOT


def code(n, head, dk, dv, packed):
    marks = packed[2 * HEADS * BLK :, :].astype(i32).astype(f32)
    rows = lax.broadcasted_iota(i32, (16, HD), 0)
    for kind, ref in enumerate((dk, dv)):
        x = ref[n * BLK : (n + 1) * BLK, :]
        peak = jnp.maximum(jnp.max(jnp.abs(x), axis=0, keepdims=True), 1e-30)
        mark = jnp.ceil(jnp.log2(peak) * 256.0)
        marks = jnp.where(rows == kind * HEADS + head, mark, marks)
        fixed = x * (jnp.exp2(mark * (-1.0 / 256.0)) * QMAX)
        at = pl.multiple_of((kind * HEADS + head) * BLK, BLK)
        packed[pl.ds(at, BLK), :] = jnp.floor(fixed + 0.5).astype(i32).astype(jnp.int16)
    packed[2 * HEADS * BLK :, :] = marks.astype(i32).astype(jnp.int16)


FAR = (4, 3, 2, 1)
NEAR = (2, 1, 0)


def far_kernel(
    lens, k_gain, cs, q, g, m_in, l_in, d_in, kv4, kv3, kv2, kv1,
    dq, lse_out, mean_out, terms, pack4, pack3, kr_out, kr, vv, krt, bias, dk, dv,
):
    head, half = pl.program_id(0), pl.program_id(1)
    kvs, packs = (kv4, kv3, kv2, kv1), (pack4, pack3)
    done = len(packs) * BLK
    place = lax.axis_index("ctx")
    base, total, opening = token_base(place, 0, half), jnp.int32(0), jnp.int32(0)
    for j in range(lens.shape[1]):
        total = total + lens[0, j]
        opening = jnp.where(base >= total, total, opening)
    reaches = opening < (place // 2) * BLK

    @pl.when((head == 0) & (half == 0))
    def _():
        terms[...] = jnp.zeros(terms.shape, f32)
        for pack in packs:
            pack[2 * HEADS * BLK :, :] = jnp.zeros((16, HD), jnp.int16)
        for part in range(2):
            fill_bias(bias, FAR, part, lens)

    @pl.when(half == 0)
    def _():
        for n, k in enumerate(FAR):
            load_block(n, k, kvs[n], cs, k_gain[...], kr, vv)
        krt[...] = jnp.transpose(kr[:done, :].astype(f32)).astype(bf16)
        kr_out[0] = kr[done:, :]

    dk[half] = jnp.zeros(dk.shape[1:], f32)
    dv[half] = jnp.zeros(dv.shape[1:], f32)

    def finish(two, e, dp, m, l, d):
        mean = d / l
        lse_out[two] = m * EXP_SCALE + jnp.log2(l)
        mean_out[two] = mean
        p = e[:done] * (1.0 / l)
        ds = (p * (dp[:done] - mean)).astype(bf16)
        dv[half] += dot(p.astype(bf16), g[two], ((1,), (0,)))
        dk[half] += dot(ds, q[two], ((1,), (0,)))
        dq[two] = dot(krt[...], ds, ((1,), (0,)))

    def products(two):
        s = dot(kr[...], q[two], ((1,), (1,))) + widen(bias.at[half], slice(None))
        return s, dot(vv[...], g[two], ((1,), (1,)))

    def near_peak(two, above):
        s, dp = products(two)
        m = m_in[two]
        gap = s - m
        e = jnp.exp2(gap * EXP_SCALE)
        l = l_in[two] + jnp.sum(e, axis=0, keepdims=True)
        d = d_in[two] + jnp.sum(e * dp, axis=0, keepdims=True)
        finish(two, e, dp, m, l, d)
        return jnp.maximum(above, jnp.max(gap, axis=0, keepdims=True))

    def any_peak(two, carry):
        s, dp = products(two)
        m_old = m_in[two]
        m = jnp.maximum(m_old, jnp.max(s, axis=0, keepdims=True))
        e = jnp.exp2((s - m) * EXP_SCALE)
        fade = jnp.exp2((m_old - m) * EXP_SCALE)
        l = l_in[two] * fade + jnp.sum(e, axis=0, keepdims=True)
        d = d_in[two] * fade + jnp.sum(e * dp, axis=0, keepdims=True)
        finish(two, e, dp, m, l, d)
        return carry

    @pl.when(reaches)
    def _():
        start = jnp.full((1, BLK), MASKED, f32)
        above = lax.fori_loop(0, GROUP // 2, near_peak, start, unroll=UNROLL)

        @pl.when(jnp.max(above) > GAP_MAX)
        def _():
            dk[half] = jnp.zeros(dk.shape[1:], f32)
            dv[half] = jnp.zeros(dv.shape[1:], f32)
            lax.fori_loop(0, GROUP // 2, any_peak, 0)

    @pl.when(jnp.logical_not(reaches))
    def _():
        lse_out[...] = m_in[...] * EXP_SCALE + jnp.log2(l_in[...])
        mean_out[...] = d_in[...] / l_in[...]
        dq[...] = jnp.zeros(dq.shape, f32)

    @pl.when(half == 1)
    def _():
        dk[0] += dk[1]
        dv[0] += dv[1]
        for n, k in enumerate(FAR[: len(packs)]):
            terms[1:2, :] = terms[1:2, :] + gain_term(k, n, kvs[n], cs, dk.at[0])
            code(n, head, dk.at[0], dv.at[0], packs[n])


def near_kernel(
    lens, q_gain, cs, q, g, lse, mean, dq_in, terms_in, q_own, q_other, kr21, kr0, kv2, kv1, kv0,
    q_grad, terms, pack2, pack1, dk_own, dv_own, kr, vv, krt, bias, dk, dv,
):
    head, half = pl.program_id(0), pl.program_id(1)
    kvs, packs = (kv2, kv1, kv0), (pack2, pack1)

    @pl.when((head == 0) & (half == 0))
    def _():
        terms[...] = terms_in[...]
        for pack in packs:
            pack[2 * HEADS * BLK :, :] = jnp.zeros((16, HD), jnp.int16)
        for part in range(2):
            fill_bias(bias, NEAR, part, lens)

    @pl.when(half == 0)
    def _():
        kr[: 2 * BLK, :] = kr21[0]
        kr[2 * BLK :, :] = kr0[0]
        for n in range(len(NEAR)):
            for part in range(2):
                at = n * BLK + part * TOK
                vv[at : at + TOK, :] = kvs[n][part, 1, 0]
        krt[...] = jnp.transpose(kr[...].astype(f32)).astype(bf16)
        dk[...] = jnp.zeros(dk.shape, f32)
        dv[...] = jnp.zeros(dv.shape, f32)

    rows = pl.ds(pl.multiple_of(half * TOK, TOK), TOK)
    cosine, sine = tables(cs[0, rows, :])
    first = half == 0

    def body(two, total):
        s = dot(kr[...], q[two], ((1,), (1,))) + widen(bias.at[half], slice(None))
        dp = dot(vv[...], g[two], ((1,), (1,)))
        p = jnp.exp2(s * EXP_SCALE - lse[two])
        ds = (p * (dp - mean[two])).astype(bf16)
        dv[...] += dot(p.astype(bf16), g[two], ((1,), (0,)))
        dk[...] += dot(ds, q[two], ((1,), (0,)))
        incoming = jnp.transpose(dq_in[two] + dot(krt[...], ds, ((1,), (0,)))) * ROOT
        for e in range(2):
            n = two * 2 + e
            x = jnp.where(first, q_own[n], q_other[n]).astype(f32)
            grad, part = unrotate(
                x, q_gain[...], cosine, sine, incoming[e * TOK : (e + 1) * TOK, :]
            )
            q_grad[0, n] = grad.astype(bf16)
            total = total + part
        return total

    total = lax.fori_loop(0, GROUP // 2, body, jnp.zeros((1, HD), f32), unroll=UNROLL)
    terms[0:1, :] = terms[0:1, :] + total

    @pl.when(half == 1)
    def _():
        for n, k in enumerate(NEAR):
            terms[1:2, :] = terms[1:2, :] + gain_term(k, n, kvs[n], cs, dk)
            if k > 0:
                code(n, head, dk, dv, packs[n])
            else:
                dk_own[0] = dk[n * BLK : (n + 1) * BLK, :]
                dv_own[0] = dv[n * BLK : (n + 1) * BLK, :]


def finish_kernel(gain, cs, kv, dk, dv, p1, p2, p3, p4, mine, other):
    gain_row = gain[...]
    packs, outs = (p1, p2, p3, p4), (mine, other)
    marks = [p[2 * HEADS * BLK :, :].astype(i32).astype(f32) for p in packs]
    for kind, ref in enumerate((dk, dv)):
        for head in range(HEADS):
            n = kind * HEADS + head
            scales = [jnp.exp2(k[n : n + 1, :] * (1.0 / 256.0)) * (1.0 / QMAX) for k in marks]
            for half in range(2):
                rows = slice(half * TOK, (half + 1) * TOK)
                total = ref[head, rows, :]
                for p, scale in zip(packs, scales):
                    at = n * BLK + half * TOK
                    total = total + p[at : at + TOK, :].astype(i32).astype(f32) * scale
                if kind == 0:
                    x = kv[half, 0, head].astype(f32)
                    cosine, sine = tables(cs[0, rows, :])
                    total, _ = unrotate(x, gain_row, cosine, sine, total * ROOT)
                outs[half][kind, head] = total.astype(bf16)


def vmem(count):
    return [pl.BlockSpec(memory_space=pltpu.VMEM)] * count


def smem(count):
    return [pl.BlockSpec(memory_space=pltpu.SMEM)] * count


def spec(shape, index):
    return pl.BlockSpec(shape, index)


PAIRS = GROUP // 2
Q_BLOCK = (PAIRS, BLK, HD)
STAT_BLOCK = (PAIRS, 1, BLK)
DQ_BLOCK = (PAIRS, HD, BLK)
RAW_BLOCK = (GROUP, TOK, HD)
KV_BLOCK = (2, 2, 1, TOK, HD)
STAT = jax.ShapeDtypeStruct((SLOTS, 1, BLK), f32)
TERMS = jax.ShapeDtypeStruct((8, HD), f32)
PACK = jax.ShapeDtypeStruct((2 * HEADS * BLK + 16, HD), jnp.int16)
OWN = jax.ShapeDtypeStruct((HEADS, BLK, HD), f32)


def by_slot(head, half):
    return (head * 2 + half, 0, 0)


def by_head(head, half):
    return (head, 0, 0)


def kv_at(head, half):
    return (0, 0, head, 0, 0)


def whole(ndim):
    return lambda head, half: (0,) * ndim


def own_raw(head, half):
    return (head, 0, 0)


def core_raw(head, half):
    return (lax.axis_index("ctx") % 2, head, 0, 0)


def block_scratch(done, blocks):
    return [
        pltpu.VMEM((blocks * BLK, HD), bf16),
        pltpu.VMEM((blocks * BLK, HD), bf16),
        pltpu.VMEM((HD, done * BLK), bf16),
        pltpu.VMEM((2, blocks * BLK, TOK), f32),
        pltpu.VMEM((done * BLK, HD), f32),
        pltpu.VMEM((done * BLK, HD), f32),
    ]


def prepare(lengths, meta, q_own, q_other, g_own, g_other, q_gain, k_gain, cs, kv):
    rows = jax.ShapeDtypeStruct((SLOTS, BLK, HD), bf16)
    return pl.pallas_call(
        prep_kernel,
        grid=(HEADS, 2),
        out_shape=[rows, rows, STAT, STAT, STAT, jax.ShapeDtypeStruct((HEADS, BLK, HD), bf16)],
        in_specs=smem(1)
        + [spec(meta.shape, whole(2))]
        + [spec((None,) + RAW_BLOCK, core_raw), spec(RAW_BLOCK, own_raw)] * 2
        + [spec((1, HD), whole(2))] * 2
        + [spec((1, BLK, HD), whole(3)), spec(KV_BLOCK, kv_at)],
        out_specs=[spec(Q_BLOCK, by_slot)] * 2
        + [spec(STAT_BLOCK, by_slot)] * 3
        + [spec((1, BLK, HD), by_head)],
        scratch_shapes=[
            pltpu.VMEM((BLK, HD), bf16),
            pltpu.VMEM((BLK, HD), bf16),
            pltpu.VMEM((2, BLK, TOK), f32),
            pltpu.VMEM((2, TOK, HD), f32),
        ],
        compiler_params=VMEM,
        cost_estimate=pl.CostEstimate(
            flops=12_000_000_000, bytes_accessed=6 << 20, transcendentals=SLOTS * BLK * BLK
        ),
        name="prepare",
    )(lengths, meta, q_own, q_other, g_own, g_other, q_gain, k_gain, cs, kv)


def far(lengths, k_gain, cs, q, g, stats, kvs):
    dq = jax.ShapeDtypeStruct((SLOTS, HD, BLK), f32)
    near_keys = jax.ShapeDtypeStruct((HEADS, 2 * BLK, HD), bf16)
    return pl.pallas_call(
        far_kernel,
        grid=(HEADS, 2),
        out_shape=[dq, STAT, STAT, TERMS, PACK, PACK, near_keys],
        in_specs=smem(1)
        + [spec((1, HD), whole(2)), spec(cs.shape, whole(3))]
        + [spec(Q_BLOCK, by_slot)] * 2
        + [spec(STAT_BLOCK, by_slot)] * 3
        + [spec(KV_BLOCK, kv_at)] * 4,
        out_specs=[spec(DQ_BLOCK, by_slot), spec(STAT_BLOCK, by_slot), spec(STAT_BLOCK, by_slot)]
        + [spec(TERMS.shape, whole(2))]
        + [spec(PACK.shape, whole(2))] * 2
        + [spec((1, 2 * BLK, HD), by_head)],
        scratch_shapes=block_scratch(2, 4)[:4] + [pltpu.VMEM((2, 2 * BLK, HD), f32)] * 2,
        compiler_params=VMEM,
        name="far",
    )(lengths, k_gain, cs, q, g, *stats, *kvs)


def near(lengths, q_gain, cs, q, g, lse, mean, dq, terms, q_own, q_other, kr21, kr0, kvs):
    row = spec((1, HD), whole(2))
    return pl.pallas_call(
        near_kernel,
        grid=(HEADS, 2),
        out_shape=[
            jax.ShapeDtypeStruct((2, HEADS * GROUP, TOK, HD), bf16),
            TERMS, PACK, PACK, OWN, OWN,
        ],
        in_specs=smem(1)
        + [row, spec((3, BLK, HD), whole(3))]
        + [spec(Q_BLOCK, by_slot)] * 2
        + [spec(STAT_BLOCK, by_slot)] * 2
        + [spec(DQ_BLOCK, by_slot), spec(TERMS.shape, whole(2))]
        + [spec((None,) + RAW_BLOCK, core_raw), spec(RAW_BLOCK, own_raw)]
        + [spec((1, 2 * BLK, HD), by_head), spec((1, BLK, HD), by_head)]
        + [spec(KV_BLOCK, kv_at)] * 3,
        out_specs=[spec((1,) + RAW_BLOCK, lambda head, half: (half, head, 0, 0))]
        + [spec(TERMS.shape, whole(2))]
        + [spec(PACK.shape, whole(2))] * 2
        + [spec((1, BLK, HD), by_head)] * 2,
        scratch_shapes=block_scratch(3, 3),
        compiler_params=VMEM,
        cost_estimate=pl.CostEstimate(
            flops=16_000_000_000, bytes_accessed=8 << 20, transcendentals=SLOTS * 3 * BLK * BLK
        ),
        name="near",
    )(lengths, q_gain, cs, q, g, lse, mean, dq, terms, q_own, q_other, kr21, kr0, *kvs)


def rope_tables(place, lens):
    chip, core = place // 2, place % 2
    k = jnp.arange(REACH + 1, dtype=i32)[:, None, None]
    half = jnp.arange(2, dtype=i32)[None, :, None]
    t = jnp.arange(TOK, dtype=i32)[None, None, :]
    index = (((chip - k) * 2 + jnp.where(half == 0, core, 1 - core)) * TOK + t).reshape(
        REACH + 1, BLK
    )
    tri = jnp.arange(lens.shape[1])
    ends = jnp.sum(jnp.where(tri[None, :] <= tri[:, None], lens[0][None, :], 0), axis=1)
    start = jnp.max(jnp.where(index[..., None] >= ends, ends, 0), axis=-1)
    lane = jnp.arange(HD, dtype=i32)
    freqs = jnp.power(1000000.0, -((lane % (HD // 2)).astype(f32) * (2.0 / HD)))
    angles = (index - start).astype(f32)[..., None] * freqs
    return jnp.where(lane < HD // 2, jnp.cos(angles), jnp.sin(angles))


def swap_cores(x):
    return lax.ppermute(x, "ctx", [(i, i ^ 1) for i in range(16)])


def shift_chips(x, k):
    return lax.ppermute(x, "ctx", [(i, i + 2 * k) for i in range(16) if 0 <= i + 2 * k < 16])


def on_device(queries, keys, values, out_grad, q_gain, k_gain, lengths, prompt_ids, grades):
    place = lax.axis_index("ctx")
    core = place % 2
    q_gain2, k_gain2 = q_gain.reshape(1, HD), k_gain.reshape(1, HD)

    kv = jnp.stack([keys, values]).transpose(2, 0, 1, 3).reshape(2, HEADS, 2, TOK, HD)
    kv = kv.transpose(0, 2, 1, 3, 4)
    kv_mine = lax.dynamic_index_in_dim(kv, core, 0, keepdims=False)
    kv_other = swap_cores(lax.dynamic_index_in_dim(kv, 1 - core, 0, keepdims=False))
    own = jnp.stack([kv_mine, kv_other])
    blocks = [own, shift_chips(own, 1), shift_chips(own, 2), None, shift_chips(own, 4)]
    blocks[3] = shift_chips(blocks[1], 2)

    heads = HEADS * GROUP
    q_t = queries.transpose(1, 0, 2).reshape(2, heads, TOK, HD)
    g_t = out_grad.transpose(1, 0, 2).reshape(2, heads, TOK, HD)
    q_other = swap_cores(lax.dynamic_index_in_dim(q_t, 1 - core, 0, keepdims=False))
    g_other = swap_cores(lax.dynamic_index_in_dim(g_t, 1 - core, 0, keepdims=False))
    cs = rope_tables(place, lengths)
    meta = jnp.stack([prompt_ids.reshape(-1), grades.reshape(-1)]).astype(f32)

    q, g, m, l, d, kr0 = prepare(
        lengths, meta, q_t, q_other, g_t, g_other, q_gain2, k_gain2, cs, own
    )
    dq, lse, mean, terms, pack4, pack3, kr21 = far(
        lengths, k_gain2, cs, q, g, (m, l, d), [blocks[k] for k in FAR]
    )
    back4, back3 = shift_chips(pack4, -4), shift_chips(pack3, -3)
    q_half, terms, pack2, pack1, dk, dv = near(
        lengths, q_gain2, cs, q, g, lse, mean, dq, terms, q_t, q_other, kr21, kr0,
        [blocks[k] for k in NEAR],
    )
    back2, back1 = shift_chips(pack2, -2), shift_chips(pack1, -1)

    q_swapped = swap_cores(q_half[1])
    first = jnp.where(core == 0, q_half[0], q_swapped)
    second = jnp.where(core == 0, q_swapped, q_half[0])
    q_grad = jnp.concatenate([first, second]).transpose(1, 0, 2)

    pair = terms[:2].reshape(1, 2 * HD)
    count = lax.axis_size("dp") * lax.axis_size("ctx")
    gathered = lax.all_to_all(
        jnp.broadcast_to(pair, (count, 2 * HD)), ("dp", "ctx"), 0, 0, tiled=True
    )
    gains = jnp.sum(gathered, axis=0)

    mine, other = pl.pallas_call(
        finish_kernel,
        out_shape=[jax.ShapeDtypeStruct((2, HEADS, TOK, HD), bf16)] * 2,
        in_specs=vmem(9),
        out_specs=vmem(2),
        compiler_params=VMEM,
        name="finish",
    )(k_gain2, cs, own, dk, dv, back1, back2, back3, back4)
    other = swap_cores(other)
    first = jnp.where(core == 0, mine, other)
    second = jnp.where(core == 0, other, mine)
    kv_grad = jnp.concatenate([first, second], axis=1).transpose(0, 2, 1, 3)
    return (q_grad, kv_grad[0], kv_grad[1], gains[:HD], gains[HD:])


def solution(mesh):
    rows = P(("dp", "ctx"), None, None)
    return jax.shard_map(
        on_device,
        mesh=mesh,
        in_specs=(rows, rows, rows, rows, P(), P(), P("dp", None), P(), P()),
        out_specs=(rows, rows, rows, P(), P()),
        check_vma=False,
    )
```
